32 devices in a mesh: groups: 2 (over y), expert: 4 (over x, core), dp: 4 (over z).
Axes of the slice: x: 2, y: 2, z: 4, core: 2. Of those that a mesh axis runs over, the one named last changes fastest.
Arguments:
- tokens: bfloat16 [1024, 4096], P(('groups', 'expert'), 'dp'), parts along dimension 0, may hold values from -6 to 6
- routes: int32 [1024, 2], P(('groups', 'expert')), parts along dimension 0, may hold values from 0 to 3, all different within a row; in each aligned block of 128 rows (0 to 127, 128 to 255, ...) at most 96 rows name the same one
- router_projection_weight: bfloat16 [4096, 4], P('dp'), may hold values from -0.09375 to 0.09375
- packed_quant_codes: int32 [4, 4096, 1536], P('expert', 'dp'), may hold values from 0 to 4095
- block_absmax_scales: float32 [4, 3, 4096, 24], P('expert', None, 'dp'), may hold values from 0.01 to 0.1
- gate_up_adapter_input: bfloat16 [4, 2, 4096, 64], P('expert', None, 'dp'), may hold values from -0.09375 to 0.09375
- gate_up_adapter_output: bfloat16 [4, 2, 64, 1536], P('expert'), may hold values from -0.75 to 0.75
- down_adapter_input: bfloat16 [4, 1536, 64], P('expert'), may hold values from -0.15625 to 0.15625
- down_adapter_output: bfloat16 [4, 64, 4096], P('expert', None, 'dp'), may hold values from -0.75 to 0.75
- cotangent: bfloat16 [1024, 4096], P(('groups', 'expert'), 'dp'), parts along dimension 0, may hold values from -6 to 6
Outputs:
- out_y: bfloat16 [1024, 4096], P(('groups', 'expert'), 'dp'), parts along dimension 0
- grad_tokens: bfloat16 [1024, 4096], P(('groups', 'expert'), 'dp'), parts along dimension 0
- grad_router: float32 [8192, 4], P(('groups', 'dp')), parts along dimension 0
- grad_gate_up_a: float32 [8, 2, 4096, 64], P(('groups', 'expert'), None, 'dp'), parts along dimension 0
- grad_gate_up_b: float32 [8, 2, 64, 1536], P(('groups', 'expert'), None, None, 'dp'), parts along dimension 0
- gradient_down_input: float32 [8, 1536, 64], P(('groups', 'expert'), 'dp'), parts along dimension 0
- gradient_down_output: float32 [8, 64, 4096], P(('groups', 'expert'), None, 'dp'), parts along dimension 0
The draws below stay inside these ranges and needn't reach their ends.
There are 2 independent parts, one for each index of `groups`. The reference program is written for one: setup_inputs(seed, part) draws one part's arguments, and reference() takes and returns one part's arrays. A program takes and returns all parts, laid end to end along the dimension named above; an argument that names none is the same for every part. Nothing has to cross between parts.
Inputs may be any that keep to these rules, and one draw needn't show every extreme that they name: `routes`: each row names 2 different experts. In each aligned block of 128 rows (the tokens of one index of expert) no expert is named by more than 96 rows, a bound that some block reaches. `packed_quant_codes`: each entry holds three NF4 codes: gate in the lowest four bits, up in the next four, down in the next four.
All inputs are finite; a program needn't handle non-finite values.
Results may differ from the reference program's by a relative error of at most 0.02.
Values may be sent and summed in bfloat16 or wider, within the bound.
No kernel may reach another device: no remote copies, remote signals or barrier semaphores. Data moves between devices by JAX's collectives and lax.ppermute only.
A program may use at most 128 MiB of HBM per device.

```python
import math
import jax
import jax.numpy as jnp
import numpy as np
from jax import lax

MODEL_WIDTH = 4096
HIDDEN_UNITS = 1536
ADAPTER_RANK = 64
BLOCK = 64
SLOTS = 2
TOK_DEV = 128
EXPERT_TOTAL = 4
CAP = 96
ROWS_IN = 384
TOKENS = 512
N_DP = 4


def set_ends(array, key, low, top_value):
    dims = array.shape
    index_at = [jax.random.randint(jax.random.fold_in(key, axis), (), 0, dims[axis]) for axis in range(len(dims))]
    array = array.at[tuple(index_at)].set(low)
    longest = dims.index(max(dims))
    index_at[longest] = (index_at[longest] + 1) % dims[longest]
    return array.at[tuple(index_at)].set(top_value)


def block_levels(key, extent, cuts, low, high):
    def one(dim, blocks):
        steps = jax.random.uniform(jax.random.fold_in(jax.random.fold_in(key, 6), dim), (blocks,), jnp.float32, low / len(cuts), high / len(cuts))
        return jnp.repeat(jnp.exp(steps), extent[dim] // blocks).reshape((-1,) + (1,) * (len(extent) - dim - 1))

    factor_of = one(*cuts[0])
    for cut in cuts[1:]:
        factor_of = factor_of * one(*cut)
    return factor_of


def routed_block(stream_key, own, number, rows, amount, top, reach, skew):
    order = jax.random.permutation(stream_key, amount)
    crowded, common = load_shares(amount, rows * top, reach, skew, True), load_shares(amount, rows * top, reach, skew, False)
    places = jnp.arange(amount)

    def named(tallies, turn):
        used = int((tallies > 0).sum())
        fixed = max(1, used // 4)
        moved = fixed + (places - fixed + turn * (used - fixed)) % max(1, amount - fixed)
        return jnp.zeros((amount,), jnp.int32).at[order[jnp.where(places < fixed, places, moved)]].set(jnp.asarray(tallies, jnp.int32))

    tallies = jnp.where(number % 4 == 0, named(crowded, number // 4), named(common, number - number // 4 - 1))
    mixed = jax.random.permutation(jax.random.fold_in(own, 3), amount)
    donor, taker = mixed[0:amount // 2 * 2:2], mixed[1:amount // 2 * 2:2]
    room = jnp.minimum(tallies[donor] - 1, reach - tallies[taker]) // 2
    room = jnp.where((donor == order[0]) | (taker == order[0]) | (tallies[taker] == 0), 0, jnp.maximum(room, 0))
    moved = jax.random.randint(jax.random.fold_in(own, 4), (amount // 2,), 0, 1 << 20) % (room + 1)
    tallies = tallies.at[donor].add(-moved).at[taker].add(moved)
    items = jnp.searchsorted(jnp.cumsum(tallies), jnp.arange(rows * top), side="right").astype(jnp.int32)
    listing = items.reshape(top, rows).T
    listing = listing[jax.random.permutation(jax.random.fold_in(own, 1), rows)]
    turn = jax.random.randint(jax.random.fold_in(own, 2), (rows, 1), 0, top)
    return jnp.take_along_axis(listing, (jnp.arange(top)[None, :] + turn) % top, axis=1)


def load_shares(number_of, total, bound, slope, full):
    loads = [(1 << 20) // math.isqrt(grade ** slope) + 1 for grade in range(1, number_of + 1)]
    largest = bound if full else min(bound, max(-(-total // number_of), total * loads[0] // sum(loads)))
    least = 1 if total - largest >= number_of - 1 else 0
    given, surplus = [largest] + [least] * (number_of - 1), total - largest - least * (number_of - 1)
    while surplus > 0:
        candidates = [i for i in range(1, number_of) if given[i] < largest] or [i for i in range(1, number_of) if given[i] < bound]
        whole, remaining = sum([loads[i] for i in candidates]), surplus
        for i in candidates:
            extra = min(bound - given[i], max(1, remaining * loads[i] // whole), surplus)
            given[i] = given[i] + extra
            surplus = surplus - extra
    return np.array(given)


def centred(stream_key, shape, spread, most, pieces=(), kind=jnp.bfloat16):
    drawn = jax.random.normal(stream_key, shape, jnp.float32) * spread
    if len(pieces) > 0:
        drawn = block_levels(stream_key, shape, pieces, -0.22, 0.18) * drawn
    return jnp.clip(drawn, min=-most, max=most).astype(kind)


def setup_inputs(seed: int = 0, part: int = 0) -> dict:
    splits = jax.random.split(jax.random.key(seed), 11)
    part_keys = jax.random.split(jax.random.fold_in(splits[10], part), 11)
    tokens = centred(part_keys[0], (TOKENS, MODEL_WIDTH), 1.0, 6.0, ((0, 4), (1, 4)))
    routes_keys = jax.random.split(jax.random.fold_in(part_keys[1], 1), TOKENS // TOK_DEV)
    routes_turns = jax.random.permutation(jax.random.fold_in(part_keys[1], 3), TOKENS // TOK_DEV)
    routes = jax.vmap(lambda own, number: routed_block(jax.random.fold_in(part_keys[1], 2), own, number, TOK_DEV, EXPERT_TOTAL, SLOTS, CAP, 2))(routes_keys, routes_turns).reshape((TOKENS, SLOTS))
    router_projection_weight = centred(splits[2], (MODEL_WIDTH, EXPERT_TOTAL), MODEL_WIDTH ** -0.5, 0.09375, ((0, 4),))
    packed_quant_codes = set_ends(jax.random.randint(splits[3], (EXPERT_TOTAL, MODEL_WIDTH, HIDDEN_UNITS), 0, 4096), jax.random.fold_in(splits[3], 1), 0, 4095).astype(jnp.int32)
    block_absmax_scales = jnp.clip(jnp.exp(math.log(0.1) - 2.3025851 * jax.random.uniform(splits[4], (EXPERT_TOTAL, 3, MODEL_WIDTH, HIDDEN_UNITS // BLOCK), jnp.float32) ** block_levels(splits[4], (EXPERT_TOTAL, 3, MODEL_WIDTH, HIDDEN_UNITS // BLOCK), ((0, 4), (2, 4)), -0.2, 0.2)), 0.01, 0.1)
    gate_up_adapter_input = centred(splits[5], (EXPERT_TOTAL, 2, MODEL_WIDTH, ADAPTER_RANK), MODEL_WIDTH ** -0.5, 0.09375, ((0, 4), (2, 4)))
    gate_up_adapter_output = centred(splits[6], (EXPERT_TOTAL, 2, ADAPTER_RANK, HIDDEN_UNITS), ADAPTER_RANK ** -0.5, 0.75, ((0, 4),))
    down_adapter_input = centred(splits[7], (EXPERT_TOTAL, HIDDEN_UNITS, ADAPTER_RANK), HIDDEN_UNITS ** -0.5, 0.15625, ((0, 4),))
    down_adapter_output = centred(splits[8], (EXPERT_TOTAL, ADAPTER_RANK, MODEL_WIDTH), ADAPTER_RANK ** -0.5, 0.75, ((0, 4), (2, 4)))
    cotangent = centred(part_keys[9], (TOKENS, MODEL_WIDTH), 1.0, 6.0, ((0, 4), (1, 4)))
    return dict(tokens=tokens, routes=routes, router_projection_weight=router_projection_weight, packed_quant_codes=packed_quant_codes, block_absmax_scales=block_absmax_scales, gate_up_adapter_input=gate_up_adapter_input, gate_up_adapter_output=gate_up_adapter_output, down_adapter_input=down_adapter_input, down_adapter_output=down_adapter_output, cotangent=cotangent)


NF4_LEVELS = (-1.0, -0.6961928009986877, -0.5250730514526367, -0.39491748809814453, -0.28444138169288635, -0.18477343022823334, -0.09105003625154495, 0.0, 0.07958029955625534, 0.16093020141124725, 0.24611230194568634, 0.33791524242401123, 0.44070982933044434, 0.5626170039176941, 0.7229568362236023, 1.0)
ADAPTER_SCALE = 0.5


def dequantize(quant_codes, scale_values):
    levels_table = jnp.asarray(NF4_LEVELS, jnp.float32)
    fields = (quant_codes % 16, (quant_codes // 16) % 16, quant_codes // 256)
    feature_rows, hidden_width = quant_codes.shape
    block_count = scale_values.shape[-1]
    result = []
    for field_index in range(3):
        values = levels_table[fields[field_index]]
        scaled = values.reshape(feature_rows, block_count, hidden_width // block_count) * scale_values[field_index][:, :, None]
        result.append(scaled.reshape(feature_rows, hidden_width).astype(jnp.bfloat16))
    return result


def block_total_sum(left, right):
    count_rows = left.shape[0]
    share_width = left.shape[1] // N_DP
    left_blocks = left.astype(jnp.float32).reshape(count_rows, N_DP, share_width)
    right_blocks = right.astype(jnp.float32).reshape(N_DP, share_width, right.shape[1])
    block_terms = jnp.einsum("rbd,bdf->rbf", left_blocks, right_blocks)
    rounded = lax.optimization_barrier(block_terms.astype(jnp.bfloat16))
    return jnp.sum(rounded.astype(jnp.float32), axis=1)


def expert_forward_pass(input_rows, slot_row_block, quant_codes, scale_values, adapter_input_map, adapter_output_map, down_input_map, down_output_map):
    gate_weight, up_weight, down_flipped_matrix = dequantize(quant_codes, scale_values)
    adapter_input = jnp.stack([block_total_sum(input_rows, adapter_input_map[0]), block_total_sum(input_rows, adapter_input_map[1])], axis=1).astype(jnp.bfloat16)
    frozen_base = jnp.stack([block_total_sum(input_rows, gate_weight), block_total_sum(input_rows, up_weight)], axis=1)
    preactivation_full = frozen_base + ADAPTER_SCALE * jnp.einsum("bvw,vwu->bvu", adapter_input.astype(jnp.float32), adapter_output_map.astype(jnp.float32))
    sigma_gate = jax.nn.sigmoid(preactivation_full[:, 0])
    silu_gate = preactivation_full[:, 0] * sigma_gate
    hidden_units = (silu_gate * preactivation_full[:, 1]).astype(jnp.bfloat16)
    hidden_lowrank = jnp.dot(hidden_units, down_input_map, preferred_element_type=jnp.float32).astype(jnp.bfloat16)
    expert_output = (jnp.dot(hidden_units, down_flipped_matrix.T, preferred_element_type=jnp.float32) + ADAPTER_SCALE * jnp.dot(hidden_lowrank, down_output_map, preferred_element_type=jnp.float32)).astype(jnp.bfloat16)
    cotangent_lowrank = block_total_sum(slot_row_block, down_output_map.T).astype(jnp.bfloat16)
    hidden_gradient = block_total_sum(slot_row_block, down_flipped_matrix) + ADAPTER_SCALE * jnp.dot(cotangent_lowrank, down_input_map.T, preferred_element_type=jnp.float32)
    grad_gate = hidden_gradient * preactivation_full[:, 1] * sigma_gate * (1.0 + preactivation_full[:, 0] * (1.0 - sigma_gate))
    grad_up = hidden_gradient * silu_gate
    preactivation_gradient = jnp.stack([grad_gate, grad_up], axis=1).astype(jnp.bfloat16)
    stacked_arrays = jnp.stack([gate_weight, up_weight]).astype(jnp.float32)
    preactivation_lowrank = jnp.einsum("vbc,bnc->vbn", preactivation_gradient.astype(jnp.float32), adapter_output_map.astype(jnp.float32)).astype(jnp.bfloat16)
    slot_gradient = (jnp.einsum("hyl,yxl->hx", preactivation_gradient.astype(jnp.float32), stacked_arrays) + ADAPTER_SCALE * jnp.einsum("csa,sga->cg", preactivation_lowrank.astype(jnp.float32), adapter_input_map.astype(jnp.float32))).astype(jnp.bfloat16)
    adapter_input_gradient = ADAPTER_SCALE * jnp.einsum("cu,cva->vua", input_rows.astype(jnp.float32), preactivation_lowrank.astype(jnp.float32))
    adapter_output_gradient = ADAPTER_SCALE * jnp.einsum("doi,dol->oil", adapter_input.astype(jnp.float32), preactivation_gradient.astype(jnp.float32))
    gradient_down_input = ADAPTER_SCALE * jnp.dot(hidden_units.T, cotangent_lowrank, preferred_element_type=jnp.float32)
    gradient_down_output = ADAPTER_SCALE * jnp.dot(hidden_lowrank.T, slot_row_block, preferred_element_type=jnp.float32)
    return expert_output, slot_gradient, adapter_input_gradient, adapter_output_gradient, gradient_down_input, gradient_down_output


def reference(tokens, routes, router_projection_weight, packed_quant_codes, block_absmax_scales, gate_up_adapter_input, gate_up_adapter_output, down_adapter_input, down_adapter_output, cotangent):
    logits = jnp.dot(tokens, router_projection_weight, preferred_element_type=jnp.float32)
    chosen = jnp.take_along_axis(logits, routes, axis=1)
    margin = chosen[:, 0] - chosen[:, 1]
    gates = jnp.stack([jax.nn.sigmoid(margin), jax.nn.sigmoid(-margin)], axis=1)
    slot_cotangent = (gates[:, :, None] * cotangent[:, None, :].astype(jnp.float32)).astype(jnp.bfloat16)
    row_total = TOKENS * SLOTS
    flat_routes = routes.reshape(-1)
    expert_mask = (flat_routes[:, None] == jnp.arange(EXPERT_TOTAL, dtype=jnp.int32)[None, :]).astype(jnp.int32)
    position = jnp.sum((jnp.cumsum(expert_mask, axis=0) - 1) * expert_mask, axis=1).astype(jnp.int32)
    lookup_levels = jnp.full((EXPERT_TOTAL, ROWS_IN), row_total, jnp.int32).at[flat_routes, position].set(jnp.arange(row_total, dtype=jnp.int32))
    pad_row = jnp.zeros((1, MODEL_WIDTH), jnp.bfloat16)
    token_row_block = jnp.concatenate([jnp.repeat(tokens, SLOTS, axis=0), pad_row], axis=0)
    cotangent_rows = jnp.concatenate([slot_cotangent.reshape(row_total, MODEL_WIDTH), pad_row], axis=0)

    def expert_wise(entry_list):
        index_vector_row, quant_codes, scale_values, adapter_input_map, adapter_output_map, down_input_map, down_output_map = entry_list
        return expert_forward_pass(token_row_block[index_vector_row], cotangent_rows[index_vector_row], quant_codes, scale_values, adapter_input_map, adapter_output_map, down_input_map, down_output_map)

    expert_output, slot_gradient, gradient_input_map, gradient_output_map, gradient_down_input, gradient_down_output = lax.map(expert_wise, (lookup_levels, packed_quant_codes, block_absmax_scales, gate_up_adapter_input, gate_up_adapter_output, down_adapter_input, down_adapter_output))
    flat_index = lookup_levels.reshape(-1)
    out_rows = jnp.zeros((row_total + 1, MODEL_WIDTH), jnp.bfloat16).at[flat_index].set(expert_output.reshape(-1, MODEL_WIDTH))[:row_total].reshape(TOKENS, SLOTS, MODEL_WIDTH)
    grad_rows = jnp.zeros((row_total + 1, MODEL_WIDTH), jnp.bfloat16).at[flat_index].set(slot_gradient.reshape(-1, MODEL_WIDTH))[:row_total].reshape(TOKENS, SLOTS, MODEL_WIDTH)
    gate_grad = jnp.sum(cotangent.astype(jnp.float32)[:, None, :] * out_rows.astype(jnp.float32), axis=2)
    out_y = jnp.sum(gates[:, :, None] * out_rows.astype(jnp.float32), axis=1).astype(jnp.bfloat16)
    logit_step = gates[:, 0] * gates[:, 1] * (gate_grad[:, 0] - gate_grad[:, 1])
    route_mask = (routes[:, :, None] == jnp.arange(EXPERT_TOTAL, dtype=jnp.int32)[None, None, :]).astype(jnp.float32)
    logit_grad = (logit_step[:, None] * (route_mask[:, 0] - route_mask[:, 1])).astype(jnp.bfloat16)
    grad_router = jnp.dot(tokens.T, logit_grad, preferred_element_type=jnp.float32)
    grad_tokens = (jnp.sum(grad_rows.astype(jnp.float32), axis=1) + jnp.dot(logit_grad, router_projection_weight.T, preferred_element_type=jnp.float32)).astype(jnp.bfloat16)
    return (out_y, grad_tokens, grad_router, gradient_input_map, gradient_output_map, gradient_down_input, gradient_down_output)
```

```python
import functools

import jax
import jax.numpy as jnp
from jax import lax
from jax.experimental import pallas as pl
from jax.experimental.pallas import tpu as pltpu
from jax.sharding import PartitionSpec as P

NF4_LEVELS = (
    -1.0,
    -0.6961928009986877,
    -0.5250730514526367,
    -0.39491748809814453,
    -0.28444138169288635,
    -0.18477343022823334,
    -0.09105003625154495,
    0.0,
    0.07958029955625534,
    0.16093020141124725,
    0.24611230194568634,
    0.3379152424240112,
    0.44070982933044434,
    0.5626170039176941,
    0.7229568362236023,
    1.0,
)
SCALE = 0.5
BF16 = jnp.bfloat16
F32 = jnp.float32
LAG = 2
INWARD = [(0, 1), (3, 2)]
MIDDLE = [(1, 2), (2, 1)]
OUTWARD = [(1, 0), (2, 3)]


def dot(left, right):
    return jnp.dot(left, right, preferred_element_type=F32)


def dot_tn(left, right):
    return lax.dot_general(left, right, (((0,), (0,)), ((), ())), preferred_element_type=F32)


def dot_nt(left, right):
    return lax.dot_general(left, right, (((1,), (1,)), ((), ())), preferred_element_type=F32)


def dequantize_kernel(code_ref, scale_ref, level_ref, spread_ref, out_ref, *, field):
    rows, width = code_ref.shape
    step = 64
    table = jnp.broadcast_to(level_ref[0:1, :], (step, 128))
    scales = scale_ref[0]
    high = scales.astype(BF16)
    rest = scales - high.astype(F32)
    middle = rest.astype(BF16)
    low = (rest - middle.astype(F32)).astype(BF16)
    for column in range(0, width, 128):
        spread = spread_ref[:, column : column + 128]
        wide = (dot(high, spread) + dot(middle, spread)) + dot(low, spread)
        for row in range(0, rows, step):
            code = (code_ref[row : row + step, column : column + 128] >> (4 * field)) & 15
            level = jnp.take_along_axis(table, code, axis=1)
            out_ref[row : row + step, column : column + 128] = (
                level * wide[row : row + step]
            ).astype(BF16)


def dequantize(codes, scales, levels, spread, field):
    features, width = codes.shape
    blocks = scales.shape[-1]
    rows = min(256, features)
    return pl.pallas_call(
        functools.partial(dequantize_kernel, field=field),
        grid=(features // rows,),
        in_specs=[
            pl.BlockSpec((rows, width), lambda i: (i, 0)),
            pl.BlockSpec((1, rows, blocks), lambda i: (field, i, 0)),
            pl.BlockSpec((8, 128), lambda i: (0, 0)),
            pl.BlockSpec((blocks, width), lambda i: (0, 0)),
        ],
        out_specs=pl.BlockSpec((rows, width), lambda i: (i, 0)),
        out_shape=jax.ShapeDtypeStruct((features, width), BF16),
        compiler_params=pltpu.CompilerParams(vmem_limit_bytes=32 * 2**20),
        cost_estimate=pl.CostEstimate(
            flops=6 * features * blocks * width, bytes_accessed=6 * features * width, transcendentals=0
        ),
    )(codes, scales, levels, spread)


def hop(value, step, count):
    return lax.ppermute(value, "expert", [(e, e ^ step) for e in range(count)])


def gather_sources(value, count):
    got = [value] + [None] * (count - 1)
    bits = [1 << b for b in range(count.bit_length() - 1)]
    for index in sorted(range(1, count), key=lambda i: bin(i).count("1")):
        low_bit = index & -index
        got[index] = hop(got[index ^ low_bit], low_bit, count)
    return got


def sum_tree(values):
    while len(values) > 1:
        values = [values[2 * i] + values[2 * i + 1] for i in range(len(values) // 2)]
    return values[0]


def sum_dp(value, parts):
    if parts & (parts - 1):
        return lax.psum(value, "dp")
    step = 1
    while step < parts:
        value = value + lax.ppermute(value, "dp", [(z, z ^ step) for z in range(parts)])
        step *= 2
    return value


def shards(
    tokens,
    routes,
    router_w,
    codes,
    scales,
    adapter_in,
    adapter_out,
    down_in,
    down_out,
    cotangent,
):
    token_count, features = tokens.shape
    slots = routes.shape[1]
    experts = router_w.shape[1]
    capacity = 3 * token_count * slots // (2 * experts)
    codes, scales = codes[0], scales[0]
    a_gate, a_up = adapter_in[0, 0], adapter_in[0, 1]
    b_gate, b_up = adapter_out[0, 0], adapter_out[0, 1]
    down_in, down_out = down_in[0], down_out[0]
    hidden_width = codes.shape[1]
    rank = a_gate.shape[1]
    blocks = scales.shape[-1]
    parts = lax.axis_size("dp")
    me = lax.axis_index("expert")
    z_index = lax.axis_index("dp")
    share = hidden_width // parts
    share_start = z_index * share

    all_tokens = gather_sources(tokens, experts)
    all_cots = gather_sources(cotangent, experts)
    routes_t = routes.T.astype(F32)
    logits = lax.dot_general(
        router_w, tokens, (((0,), (1,)), ((), ())), preferred_element_type=F32
    )
    logits = sum_dp(logits, parts)
    number = lax.broadcasted_iota(jnp.int32, (experts, 1), 0).astype(F32)
    chosen = [
        jnp.sum(jnp.where(routes_t[k : k + 1] == number, logits, 0.0), axis=0, keepdims=True)
        for k in range(2)
    ]
    margin = chosen[0] - chosen[1]
    gates = jnp.concatenate([jax.nn.sigmoid(margin), jax.nn.sigmoid(-margin)], axis=0)
    all_routes = gather_sources(routes_t, experts)
    all_gates = gather_sources(gates, experts)

    levels = jnp.zeros((8, 128), F32).at[:, :16].set(jnp.asarray(NF4_LEVELS, F32)[None])
    spread = (
        lax.broadcasted_iota(jnp.int32, (blocks, hidden_width), 0)
        == lax.broadcasted_iota(jnp.int32, (blocks, hidden_width), 1) // (hidden_width // blocks)
    ).astype(BF16)
    weights = [dequantize(codes, scales, levels, spread, field) for field in range(3)]

    me_f = me.astype(F32)
    before = (
        lax.broadcasted_iota(jnp.int32, (token_count, token_count), 0)
        < lax.broadcasted_iota(jnp.int32, (token_count, token_count), 1)
    ).astype(BF16)
    row_number = lax.broadcasted_iota(jnp.int32, (capacity, 1), 0).astype(F32)

    per_chunk = max(1, experts // 4)
    order = [list(range(i, i + per_chunk)) for i in range(0, experts, per_chunk)]
    if len(order) == 4:
        order = [order[0], order[2], order[3], order[1]]
    picks = {}
    row_gate = {}

    def build_picks(i):
        first = all_routes[i][0:1] == me_f
        second = all_routes[i][1:2] == me_f
        mine = first | second
        place = dot(jnp.broadcast_to(mine.astype(BF16), (8, token_count)), before)[0:1]
        pick = mine & (place == row_number)
        gate = jnp.where(first, all_gates[i][0:1], all_gates[i][1:2])
        picks[i] = pick
        row_gate[i] = jnp.sum(jnp.where(pick, gate, 0.0), axis=1, keepdims=True)

    chunk_x, chunk_c = {}, {}

    def unit_term(n, j):
        if j == 0:
            for i in order[n]:
                build_picks(i)
            chunk_x[n] = jnp.concatenate(
                [dot(picks[i].astype(BF16), all_tokens[i]).astype(BF16) for i in order[n]], axis=0
            )
            low = dot(chunk_x[n], jnp.concatenate([a_gate, a_up], axis=1))
            return jnp.concatenate([dot(chunk_x[n], weights[0]).astype(BF16), low.astype(BF16)], axis=1)
        if j == 1:
            return dot(chunk_x[n], weights[1]).astype(BF16)
        chunk_c[n] = jnp.concatenate(
            [dot(picks[i].astype(BF16), all_cots[i]).astype(BF16) for i in order[n]], axis=0
        )
        low = dot_nt(chunk_c[n], down_out)
        return jnp.concatenate([dot(chunk_c[n], weights[2]).astype(BF16), low.astype(BF16)], axis=1)

    saved = {}
    own_parts, back = [], {}
    gate_terms = {}

    def finish(n, sums):
        gate_sum, up_sum, grad_sum = sums
        low_gate = gate_sum[:, hidden_width : hidden_width + rank]
        low_up = gate_sum[:, hidden_width + rank :]
        cot_low = grad_sum[:, hidden_width:]
        gate_of = jnp.concatenate([row_gate[i] for i in order[n]], axis=0)
        g = gate_sum[:, :hidden_width].astype(F32) + SCALE * dot(low_gate, b_gate)
        u = up_sum.astype(F32) + SCALE * dot(low_up, b_up)
        h = grad_sum[:, :hidden_width].astype(F32) + SCALE * dot_nt(cot_low, down_in)
        sigma = jax.nn.sigmoid(g)
        silu = g * sigma
        hidden = (silu * u).astype(BF16)
        gate_grad = jnp.sum(hidden.astype(F32) * h, axis=1, keepdims=True)
        hg = h * gate_of
        grad_gate = (hg * u * sigma * (1.0 + g * (1.0 - sigma))).astype(BF16)
        grad_up = (hg * silu).astype(BF16)
        hidden_low = dot(hidden, down_in).astype(BF16)
        out = (dot_nt(hidden, weights[2]) + SCALE * dot(hidden_low, down_out)) * gate_of
        low_g = dot_nt(grad_gate, b_gate).astype(BF16)
        low_u = dot_nt(grad_up, b_up).astype(BF16)
        slot = (dot_nt(grad_gate, weights[0]) + dot_nt(grad_up, weights[1])) + SCALE * (
            dot_nt(low_g, a_gate) + dot_nt(low_u, a_up)
        )
        both = jnp.concatenate([out.astype(BF16), slot.astype(BF16)], axis=1)
        saved[n] = (
            low_gate,
            low_up,
            lax.dynamic_slice_in_dim(grad_gate, share_start, share, 1),
            lax.dynamic_slice_in_dim(grad_up, share_start, share, 1),
            lax.dynamic_slice_in_dim(hidden, share_start, share, 1),
            (cot_low.astype(F32) * gate_of).astype(BF16),
            (hidden_low.astype(F32) * gate_of).astype(BF16),
            low_g,
            low_u,
        )
        dense = []
        for at, i in enumerate(order[n]):
            rows = slice(at * capacity, (at + 1) * capacity)
            dense.append(dot_tn(picks[i].astype(BF16), both[rows]).astype(BF16))
            sign = jnp.where(all_routes[i][0:1] == me_f, 1.0, -1.0)
            gate_terms[i] = sign * jnp.sum(
                jnp.where(picks[i], gate_grad[rows], 0.0), axis=0, keepdims=True
            )
        return dense

    def send_back(n, dense):
        for at, i in enumerate(order[n]):
            back[i] = dense[at] if i == 0 else hop(dense[at], i, experts)

    chunks = len(order)
    units = [(n, j) for n in range(chunks) for j in range(3)]
    total = len(units)
    if parts == 4:
        end = (z_index == 0) | (z_index == 3)
        term, came, inner, crossed, whole, outer, done = {}, {}, {}, {}, {}, {}, {}
        ready = {}
        for t in range(total + 3 * LAG + LAG):
            ka, kb, kc, kd = t, t - LAG, t - 2 * LAG, t - 3 * LAG
            live = {}
            if ka < total:
                live["a"] = unit_term(*units[ka])
            if 0 <= kb < total:
                live["b"] = term[kb] + came[kb]
            if 0 <= kc < total:
                live["c"] = inner[kc] + crossed[kc]
            if 0 <= kd < total:
                live["d"] = jnp.where(end, outer[kd], whole[kd])
            if t in ready:
                live["r"] = ready[t][1]
            live = lax.optimization_barrier(live)
            if "a" in live:
                term[ka] = live["a"]
                came[ka] = lax.ppermute(live["a"], "dp", INWARD)
            if "b" in live:
                inner[kb] = live["b"]
                crossed[kb] = lax.ppermute(live["b"], "dp", MIDDLE)
            if "c" in live:
                whole[kc] = live["c"]
                outer[kc] = lax.ppermute(live["c"], "dp", OUTWARD)
            if "d" in live:
                done[kd] = live["d"]
                if kd % 3 == 2:
                    n = kd // 3
                    dense = finish(n, [done[3 * n + j] for j in range(3)])
                    if t + 1 < total + 3 * LAG:
                        ready[t + 1] = (n, dense)
                    else:
                        send_back(n, dense)
            if "r" in live:
                send_back(ready[t][0], live["r"])
    else:
        for n in range(chunks):
            sums = [lax.psum(unit_term(n, j), "dp") for j in range(3)]
            send_back(n, finish(n, sums))

    signed = jnp.concatenate([gate_terms[i] for i in range(experts)], axis=0)
    gathered = gather_sources(signed, experts)
    lines = []
    router_terms = []
    for i in range(experts):
        margin_grad = sum_tree([gathered[j][i ^ j : (i ^ j) + 1] for j in range(experts)])
        step = all_gates[i][0:1] * all_gates[i][1:2] * margin_grad
        line = step * (
            (all_routes[i][0:1] == number).astype(F32) - (all_routes[i][1:2] == number).astype(F32)
        )
        lines.append(line.astype(BF16))
        router_terms.append(
            lax.dot_general(
                all_tokens[i], lines[i], (((0,), (1,)), ((), ())), preferred_element_type=F32
            )
        )
    grad_router = sum_tree(router_terms)

    out_y = sum_tree([back[i][:, :features].astype(F32) for i in range(experts)]).astype(BF16)
    slot_sum = sum_tree([back[i][:, features:].astype(F32) for i in range(experts)])
    grad_tokens = (
        slot_sum
        + lax.dot_general(lines[0], router_w, (((0,), (1,)), ((), ())), preferred_element_type=F32)
    ).astype(BF16)

    def stacked(values):
        return jnp.concatenate(values, axis=0)

    s = [stacked([saved[n][f] for n in range(chunks)]) for f in range(9)]
    x_all = stacked([chunk_x[n] for n in range(chunks)])
    c_all = stacked([chunk_c[n] for n in range(chunks)])
    grad_a = SCALE * jnp.stack([dot_tn(x_all, s[7]), dot_tn(x_all, s[8])])
    grad_b = SCALE * jnp.stack([dot_tn(s[0], s[2]), dot_tn(s[1], s[3])])
    grad_di = SCALE * dot_tn(s[4], s[5])
    grad_do = SCALE * dot_tn(s[6], c_all)
    return out_y, grad_tokens, grad_router, grad_a[None], grad_b[None], grad_di[None], grad_do[None]


def solution(mesh):
    in_specs = (
        P(("groups", "expert"), "dp"),
        P(("groups", "expert"), None),
        P("dp", None),
        P("expert", "dp", None),
        P("expert", None, "dp", None),
        P("expert", None, "dp", None),
        P("expert", None, None, None),
        P("expert", None, None),
        P("expert", None, "dp"),
        P(("groups", "expert"), "dp"),
    )
    out_specs = (
        P(("groups", "expert"), "dp"),
        P(("groups", "expert"), "dp"),
        P(("groups", "dp"), None),
        P(("groups", "expert"), None, "dp", None),
        P(("groups", "expert"), None, None, "dp"),
        P(("groups", "expert"), "dp", None),
        P(("groups", "expert"), None, "dp"),
    )
    return jax.shard_map(shards, mesh=mesh, in_specs=in_specs, out_specs=out_specs, check_vma=False)
```

```python
import functools

import jax
import jax.numpy as jnp
import numpy as np
from jax import lax
from jax.experimental import pallas as pl
from jax.experimental.pallas import tpu as pltpu
from jax.sharding import PartitionSpec as P

NF4_LEVELS = (
    -1.0,
    -0.6961928009986877,
    -0.5250730514526367,
    -0.39491748809814453,
    -0.28444138169288635,
    -0.18477343022823334,
    -0.09105003625154495,
    0.0,
    0.07958029955625534,
    0.16093020141124725,
    0.24611230194568634,
    0.3379152424240112,
    0.44070982933044434,
    0.5626170039176941,
    0.7229568362236023,
    1.0,
)
SCALE = 0.5
BF16 = jnp.bfloat16
F32 = jnp.float32
LAG = 2
LAST_COST = pl.CostEstimate(flops=6 * 10**9, bytes_accessed=16 * 10**6, transcendentals=0)
NO_COST = pl.CostEstimate(flops=0, bytes_accessed=0, transcendentals=0)
INWARD = [(0, 1), (3, 2)]
MIDDLE = [(1, 2), (2, 1)]
OUTWARD = [(1, 0), (2, 3)]


def dot(left, right):
    return jnp.dot(left, right, preferred_element_type=F32)


def dot_tn(left, right):
    return lax.dot_general(left, right, (((0,), (0,)), ((), ())), preferred_element_type=F32)


def dot_nt(left, right):
    return lax.dot_general(left, right, (((1,), (1,)), ((), ())), preferred_element_type=F32)


def dequantize_kernel(code_ref, scale_ref, level_ref, spread_ref, *refs, field):
    out_ref = refs[-1]
    rows, width = code_ref.shape
    step = 64
    table = jnp.broadcast_to(level_ref[0:1, :], (step, 128))
    scales = scale_ref[0]
    high = scales.astype(BF16)
    rest = scales - high.astype(F32)
    middle = rest.astype(BF16)
    low = (rest - middle.astype(F32)).astype(BF16)
    for column in range(0, width, 128):
        spread = spread_ref[:, column : column + 128]
        wide = (dot_tn(high, spread) + dot_tn(middle, spread)) + dot_tn(low, spread)
        for row in range(0, rows, step):
            code = (code_ref[row : row + step, column : column + 128] >> (4 * field)) & 15
            level = jnp.take_along_axis(table, code, axis=1)
            out_ref[row : row + step, column : column + 128] = (
                level * wide[row : row + step]
            ).astype(BF16)


def dequantize(codes, scales, levels, spread, field, *after):
    features, width = codes.shape
    blocks = scales.shape[1]
    rows = min(256, features)
    return pl.pallas_call(
        functools.partial(dequantize_kernel, field=field),
        grid=(features // rows,),
        in_specs=[
            pl.BlockSpec((rows, width), lambda i: (i, 0)),
            pl.BlockSpec((1, blocks, rows), lambda i: (field, 0, i)),
            pl.BlockSpec((8, 128), lambda i: (0, 0)),
            pl.BlockSpec((blocks, width), lambda i: (0, 0)),
        ]
        + [pl.BlockSpec(memory_space=pl.ANY)] * len(after),
        out_specs=pl.BlockSpec((rows, width), lambda i: (i, 0)),
        out_shape=jax.ShapeDtypeStruct((features, width), BF16),
        compiler_params=pltpu.CompilerParams(vmem_limit_bytes=(12 if after else 56) * 2**20),
        cost_estimate=NO_COST,
    )(codes, scales, levels, spread, *after)


def call(body, args, after, shapes, piped=False):
    smem = pl.BlockSpec(memory_space=pltpu.SMEM)
    count = len(args)
    extra = len(after)

    def whole(shape):
        if piped:
            return pl.BlockSpec(shape, lambda i: (0,) * len(shape))
        return pl.BlockSpec(memory_space=pltpu.VMEM)

    def kernel(*refs):
        body(list(refs[:count]), list(refs[count + extra :]))

    out = pl.pallas_call(
        kernel,
        grid=(1,) if piped else (),
        in_specs=[smem if a.dtype == jnp.int32 else whole(a.shape) for a in args]
        + [pl.BlockSpec(memory_space=pl.ANY)] * extra,
        out_specs=[whole(shape) for shape, _ in shapes],
        out_shape=[jax.ShapeDtypeStruct(shape, dtype) for shape, dtype in shapes],
        compiler_params=pltpu.CompilerParams(vmem_limit_bytes=(24 if piped else 10) * 2**20),
        cost_estimate=NO_COST,
    )(*args, *after)
    return list(out)


def run_step(end, kind, unit, pairs, pack, logits_of, after):
    args, shapes, count = [end], [], 0
    if kind is not None:
        rows, blocks, weight, low = unit
        if kind == 1:
            args.append(rows)
            count = rows.shape[0]
        else:
            features = weight.shape[0]
            count = sum(pick.shape[0] for pick, _, _ in blocks)
            for pick, block, _ in blocks:
                args += [pick, block]
            shapes.append(((count, features), BF16))
        args += [weight, low]
        shapes.append(((count, weight.shape[1] + low.shape[-2]), BF16))
    for name in pairs:
        args += list(pairs[name])
        shapes.append((pairs[name][0].shape, BF16))
    if pack is not None:
        args += list(pack)
        tokens, _, routes = pack
        shapes.append(((tokens.shape[0] + routes.shape[0], 2 * tokens.shape[1]), BF16))
    if logits_of is not None:
        router, packs = logits_of
        token_count = packs[0].shape[0] - 16
        args += [router] + packs
        shapes.append(((router.shape[0], token_count * len(packs)), F32))

    def body(ins, outs):
        is_end = ins.pop(0)[0]
        term = None
        if kind is not None:
            if kind == 1:
                rows_ref = ins.pop(0)
            else:
                rows_ref = outs.pop(0)
                found = []
                for pick, block, at in blocks:
                    pick_ref, block_ref = ins.pop(0), ins.pop(0)
                    found.append(
                        dot(pick_ref[...], block_ref[: pick.shape[1], at : at + rows_ref.shape[1]])
                    )
                rows_ref[...] = (jnp.concatenate(found, axis=0) if len(found) > 1 else found[0]).astype(
                    BF16
                )
            weight_ref, low_ref = ins.pop(0), ins.pop(0)
            term = outs.pop(0)
            width = weight_ref.shape[1]
            for column in range(0, width, 512):
                tile = slice(column, column + 512)
                term[:, tile] = dot(rows_ref[...], weight_ref[:, tile]).astype(BF16)
            low_map = low_ref[...] if kind == 2 else low_ref[kind]
            term[:, width:] = dot_nt(rows_ref[...], low_map).astype(BF16)
        for name in pairs:
            left, right, out = ins.pop(0), ins.pop(0), outs.pop(0)
            if name == "b" or (name == "c" and term is None):
                out[...] = (left[...].astype(F32) + right[...].astype(F32)).astype(BF16)
            elif name == "c":

                @pl.when(is_end == 1)
                def _(out=out):
                    out[...] = term[...]

                @pl.when(is_end == 0)
                def _(out=out, left=left, right=right):
                    out[...] = (left[...].astype(F32) + right[...].astype(F32)).astype(BF16)

            else:

                @pl.when(is_end == 1)
                def _(out=out, right=right):
                    out[...] = right[...]

                @pl.when(is_end == 0)
                def _(out=out, left=left):
                    out[...] = left[...]

        if pack is not None:
            tokens_ref, cots_ref, routes_ref, out = ins.pop(0), ins.pop(0), ins.pop(0), outs.pop(0)
            top, left = tokens_ref.shape
            out[:top, :left] = tokens_ref[...]
            out[:top, left:] = cots_ref[...]
            out[top:, : routes_ref.shape[1]] = routes_ref[...]
        if logits_of is not None:
            router_ref, out = ins.pop(0), outs.pop(0)
            features = router_ref.shape[1]
            for number in range(len(packs)):
                block = ins.pop(0)
                out[:, number * token_count : (number + 1) * token_count] = dot_nt(
                    router_ref[...], block[:token_count, :features]
                )

    return call(body, args, after, shapes)


def middle_shapes(rows, hidden_width, rank, sources, tokens):
    wide, low = ((rows, hidden_width), BF16), ((rows, rank), BF16)
    return [wide, wide, wide] + [low] * 7 + [((rows, 1), F32), ((sources, tokens), F32)]


def middle_body(ins, outs):
    gate_ref, up_ref, cot_ref, gates_ref, signs_ref, maps, down_ref = ins[:7]
    picks_ref = ins[7:]
    sources = len(picks_ref)
    rows = gate_ref.shape[0]
    cap = rows // sources
    hidden_width = maps.shape[2]
    hidden_ref, grad_gate_ref, grad_up_ref, hl_ref, lg_ref, lu_ref, hlg_ref, clg_ref = outs[:8]
    ag_ref, au_ref, gate_out, signed_ref = outs[8:]
    ag_ref[...] = gate_ref[:, hidden_width:]
    au_ref[...] = up_ref[:, hidden_width:]
    chosen = [pick[...].astype(F32) for pick in picks_ref]
    gate = [jnp.sum(chosen[i] * gates_ref[i : i + 1, :], axis=1, keepdims=True) for i in range(sources)]
    gate = jnp.concatenate(gate, axis=0) if sources > 1 else gate[0]
    gate_out[...] = gate
    cot_low = cot_ref[:, hidden_width:]
    total = jnp.zeros((rows, 1), F32)
    step = 512
    for column in range(0, hidden_width, step):
        tile = slice(column, column + step)
        g = gate_ref[:, tile].astype(F32) + SCALE * dot(gate_ref[:, hidden_width:], maps[0, :, tile])
        u = up_ref[:, tile].astype(F32) + SCALE * dot(up_ref[:, hidden_width:], maps[1, :, tile])
        h = cot_ref[:, tile].astype(F32) + SCALE * dot(cot_low, down_ref[:, tile])
        sigma = jax.nn.sigmoid(g)
        silu = g * sigma
        hidden = (silu * u).astype(BF16)
        total = total + jnp.sum(hidden.astype(F32) * h, axis=1, keepdims=True)
        h = h * gate
        hidden_ref[:, tile] = hidden
        grad_gate_ref[:, tile] = (h * u * sigma * (1.0 + g * (1.0 - sigma))).astype(BF16)
        grad_up_ref[:, tile] = (h * silu).astype(BF16)
    hidden_low = dot_nt(hidden_ref[...], down_ref[...]).astype(BF16)
    hl_ref[...] = hidden_low
    hlg_ref[...] = (hidden_low.astype(F32) * gate).astype(BF16)
    clg_ref[...] = (cot_low.astype(F32) * gate).astype(BF16)
    lg_ref[...] = dot_nt(grad_gate_ref[...], maps[0]).astype(BF16)
    lu_ref[...] = dot_nt(grad_up_ref[...], maps[1]).astype(BF16)
    for i in range(sources):
        line = jnp.sum(chosen[i] * total[i * cap : (i + 1) * cap], axis=0, keepdims=True)
        signed_ref[i : i + 1, :] = line * signs_ref[i : i + 1, :]


def run_middle(head, picks, after):
    rows, maps = head[0].shape[0], head[5]
    shapes = middle_shapes(rows, maps.shape[2], maps.shape[1], len(picks), picks[0].shape[1])
    return call(middle_body, head + picks, after, shapes)


def run_back(share_start, share, head, mid, rows_x, rows_c, weights, adapter_in_t, down_out, picks, totals, after, cost):
    rows, hidden_width = rows_x.shape[0], weights[0].shape[1]
    rank, features = down_out.shape
    sources = len(picks)
    cap = rows // sources
    width = hidden_width if share % 128 else share
    tile = min(256, features)
    tokens = picks[0].shape[1]

    def fixed(value):
        return pl.BlockSpec(value.shape, lambda i, n=value.ndim: (0,) * n)

    last = pl.BlockSpec((rows, tile), lambda i: (0, i))
    lines = pl.BlockSpec((tile, hidden_width), lambda i: (i, 0))
    low = pl.BlockSpec((rank, tile), lambda i: (0, i))
    pair = pl.BlockSpec((2, rank, tile), lambda i: (0, 0, i))
    total_specs = [
        pair,
        pl.BlockSpec((2, rank, width), lambda i: (0, 0, 0)),
        pl.BlockSpec((rank, width), lambda i: (0, 0)),
        low,
    ]
    fused = mid is None
    lead = head if fused else list(mid)
    inner = middle_shapes(rows, hidden_width, rank, sources, tokens)
    args = [share_start] + lead + [rows_x, rows_c] + list(weights) + [adapter_in_t, down_out]
    args += picks + totals + after
    specs = [pl.BlockSpec(memory_space=pltpu.SMEM)] + [fixed(value) for value in lead]
    specs += [last, last, lines, lines, lines, pair, low] + [fixed(pick) for pick in picks]
    specs += total_specs[: len(totals)] + [pl.BlockSpec(memory_space=pl.ANY)] * len(after)
    shapes = [((2, tokens, features), BF16)] * sources
    shapes += [((2, rank, features), F32), ((2, rank, width), F32), ((rank, width), F32), ((rank, features), F32)]
    out_specs = [pl.BlockSpec((2, tokens, tile), lambda i: (0, 0, i))] * sources + total_specs
    if fused:
        shapes.append(inner[-1])
        out_specs.append(pl.BlockSpec(inner[-1][0], lambda i: (0, 0)))
    given = len(totals)
    led = 1 + len(lead)

    def body(*refs):
        start = pl.multiple_of(refs[0][0], 128) if share % 128 == 0 else 0
        x_ref, c_ref, wg, wu, wd, maps, down_ref = refs[led : led + 7]
        picks_ref = refs[led + 7 : led + 7 + sources]
        old = refs[led + 7 + sources : led + 7 + sources + given]
        outs = refs[len(args) :]
        backs, new = outs[:sources], outs[sources : sources + 4]
        middle = refs[1:led]
        if fused:
            middle = outs[sources + 5 :]

            @pl.when(pl.program_id(0) == 0)
            def _():
                middle_body(list(refs[1:led]) + list(picks_ref), list(middle) + [outs[sources + 4]])

        h_ref, gg_ref, gu_ref, hl_ref, lg_ref, lu_ref, hlg_ref, clg_ref, ag_ref, au_ref, gate_ref = middle
        out = dot_nt(h_ref[...], wd[...]) + SCALE * dot(hl_ref[...], down_ref[...])
        slot = (dot_nt(gg_ref[...], wg[...]) + dot_nt(gu_ref[...], wu[...])) + SCALE * (
            dot(lg_ref[...], maps[0]) + dot(lu_ref[...], maps[1])
        )
        for which, value in enumerate((out * gate_ref[...], slot)):
            for i in range(sources):
                part = value[i * cap : (i + 1) * cap].astype(BF16)
                backs[i][which] = dot_tn(picks_ref[i][...], part).astype(BF16)

        def add(which, index, value):
            value = SCALE * value
            if given:
                value = value + old[which][index]
            new[which][index] = value

        add(0, 0, dot_tn(lg_ref[...], x_ref[...]))
        add(0, 1, dot_tn(lu_ref[...], x_ref[...]))
        add(3, ..., dot_tn(hlg_ref[...], c_ref[...]))

        @pl.when(pl.program_id(0) == 0)
        def _():
            columns = pl.ds(start, width)
            add(1, 0, dot_tn(ag_ref[...], gg_ref[:, columns]))
            add(1, 1, dot_tn(au_ref[...], gu_ref[:, columns]))
            add(2, ..., dot_tn(clg_ref[...], h_ref[:, columns]))

    out = pl.pallas_call(
        body,
        grid=(features // tile,),
        in_specs=specs,
        out_specs=out_specs,
        out_shape=[jax.ShapeDtypeStruct(shape, dtype) for shape, dtype in shapes],
        scratch_shapes=[pltpu.VMEM(shape, dtype) for shape, dtype in inner[:-1]] if fused else [],
        compiler_params=pltpu.CompilerParams(vmem_limit_bytes=20 * 2**20),
        cost_estimate=cost,
    )(*args)
    return list(out[:sources]), list(out[sources : sources + 4]), list(out[sources + 4 :])


def run_end(backs, packs, gathered, gates, routes, router_t, after):
    token_count = backs[0].shape[1]
    experts, features = router_t.shape
    args = backs + packs + gathered + [gates, routes, router_t]
    shapes = [((token_count, features), BF16), ((token_count, features), BF16), ((experts, features), F32)]

    def body(ins, outs):
        backs_ref, packs_ref, gathered_ref = ins[:experts], ins[experts : 2 * experts], ins[2 * experts : 3 * experts]
        gates_ref, routes_ref, router_ref = ins[3 * experts :]
        number = lax.broadcasted_iota(jnp.int32, (experts, 1), 0).astype(F32)
        terms, first_line = [], None
        for i in range(experts):
            at = slice(i * token_count, (i + 1) * token_count)
            margin = sum_tree([gathered_ref[j][i ^ j : (i ^ j) + 1, :] for j in range(experts)])
            step = gates_ref[0:1, at] * gates_ref[1:2, at] * margin
            line = step * (
                (routes_ref[0:1, at] == number).astype(F32) - (routes_ref[1:2, at] == number).astype(F32)
            )
            line = line.astype(BF16)
            first_line = line if i == 0 else first_line
            terms.append(dot(line, packs_ref[i][:token_count, :features]))
        outs[2][...] = sum_tree(terms)
        outs[0][...] = sum_tree([back[0].astype(F32) for back in backs_ref]).astype(BF16)
        outs[1][...] = (
            sum_tree([back[1].astype(F32) for back in backs_ref])
            + dot_tn(first_line, router_ref[...])
        ).astype(BF16)

    return call(body, args, after, shapes, True)


def hop(value, step, count):
    return lax.ppermute(value, "expert", [(e, e ^ step) for e in range(count)])


def gather_direct(value, count):
    return [value] + [hop(value, step, count) for step in range(1, count)]


def gather_sources(value, count):
    got = [value] + [None] * (count - 1)
    bits = [1 << b for b in range(count.bit_length() - 1)]
    for index in sorted(range(1, count), key=lambda i: bin(i).count("1")):
        low_bit = index & -index
        got[index] = hop(got[index ^ low_bit], low_bit, count)
    return got


def sum_tree(values):
    while len(values) > 1:
        values = [values[2 * i] + values[2 * i + 1] for i in range(len(values) // 2)]
    return values[0]


def sum_dp(value, parts):
    if parts & (parts - 1):
        return lax.psum(value, "dp")
    step = 1
    while step < parts:
        value = value + lax.ppermute(value, "dp", [(z, z ^ step) for z in range(parts)])
        step *= 2
    return value


def shards(
    tokens,
    routes,
    router_w,
    codes,
    scales,
    adapter_in,
    adapter_out,
    down_in,
    down_out,
    cotangent,
):
    token_count, features = tokens.shape
    slots = routes.shape[1]
    experts = router_w.shape[1]
    capacity = 3 * token_count * slots // (2 * experts)
    codes, scales_t = codes[0], jnp.swapaxes(scales[0], 1, 2)
    adapter_in_t = jnp.swapaxes(adapter_in[0], 1, 2)
    adapter_out, down_out = adapter_out[0], down_out[0]
    down_in_t = down_in[0].T
    router_t = router_w.T
    hidden_width = codes.shape[1]
    blocks = scales_t.shape[1]
    parts = lax.axis_size("dp")
    me = lax.axis_index("expert").astype(F32)
    z_index = lax.axis_index("dp")
    share = hidden_width // parts
    share_start = (z_index * share).astype(jnp.int32).reshape(1)
    end = ((z_index == 0) | (z_index == parts - 1)).astype(jnp.int32).reshape(1)
    number = lax.broadcasted_iota(jnp.int32, (experts, 1), 0).astype(F32)

    table = np.zeros((8, 128), np.float32)
    table[:, :16] = np.asarray(NF4_LEVELS, np.float32)
    levels = jnp.asarray(table)
    block_of = np.arange(hidden_width) // (hidden_width // blocks)
    spread = jnp.asarray(np.arange(blocks)[:, None] == block_of[None, :], BF16)
    before = jnp.asarray(np.arange(token_count)[:, None] < np.arange(token_count)[None, :], BF16)
    row_number = jnp.asarray(np.arange(capacity)[:, None], F32)
    weights = [dequantize(codes, scales_t, levels, spread, 0), None, None]

    per_chunk = max(1, experts // 4)
    order = [list(range(i, i + per_chunk)) for i in range(0, experts, per_chunk)]
    if len(order) == 4:
        order = [order[0], order[2], order[3], order[1]]

    def picks_of(first, second):
        mine = (first == me) | (second == me)
        pad = jnp.concatenate([mine, mine, mine, mine, mine, mine, mine, mine], axis=0)
        place = dot(pad[: max(8, mine.shape[0])].astype(BF16), before)
        return [
            (mine[i : i + 1] & (place[i : i + 1] == row_number)).astype(BF16) for i in range(mine.shape[0])
        ]

    routes_t = routes.T.astype(F32)
    picks = picks_of(routes_t[0:1], routes_t[1:2])
    routes_pad = jnp.pad(routes_t.astype(BF16), ((0, 14), (0, 0)))
    packs, chunk_x, chunk_c, shared = [], {}, {}, {}

    def spread_start(packed):
        packs[:] = gather_sources(packed, experts)
        rows = [pack[token_count : token_count + 2, :token_count].astype(F32) for pack in packs]
        shared["routes"] = jnp.concatenate(rows, axis=1)
        if experts > 1:
            first = jnp.concatenate([row[0:1] for row in rows[1:]], axis=0)
            second = jnp.concatenate([row[1:2] for row in rows[1:]], axis=0)
            picks[1:] = picks_of(first, second)

    def settle_gates(logits):
        logits = sum_dp(logits, parts)
        all_routes = shared["routes"]
        chosen = [
            jnp.sum(jnp.where(all_routes[k : k + 1] == number, logits, 0.0), axis=0, keepdims=True)
            for k in range(2)
        ]
        margin = chosen[0] - chosen[1]
        gates = jnp.concatenate([jax.nn.sigmoid(margin), jax.nn.sigmoid(-margin)], axis=0)
        shared["gates"] = gates
        first = all_routes[0:1] == me
        shared["mine"] = jnp.where(first, gates[0:1], gates[1:2]).reshape(experts, token_count)
        shared["signs"] = jnp.where(first, 1.0, -1.0).reshape(experts, token_count)

    def step(n, j, pairs, after, logits=False):
        kind, unit, pack = None, None, None
        if n is not None:
            kind = j
            if weights[j] is None:
                weights[j] = dequantize(codes, scales_t, levels, spread, j, *after)
            early = not packs
            if j == 0:
                taken = [(picks[i], tokens if early else packs[i], 0) for i in order[n]]
                unit = (None, taken, weights[0], adapter_in_t)
            elif j == 1:
                unit = (chunk_x[n], None, weights[1], adapter_in_t)
            else:
                unit = (None, [(picks[i], packs[i], features) for i in order[n]], weights[2], down_out)
            if early:
                pack = (tokens, cotangent, routes_pad)
        logits_of = (router_t, packs) if logits else None
        out = run_step(end, kind, unit, pairs, pack, logits_of, after)
        if logits:
            settle_gates(out.pop())
        if pack is not None:
            spread_start(out.pop())
        term = None
        if kind is not None:
            if kind == 0:
                chunk_x[n] = out.pop(0)
            elif kind == 2:
                chunk_c[n] = out.pop(0)
            term = out.pop(0)
        return term, dict(zip(pairs, out))

    back, totals, signed = {}, [], {}

    def finish(n, sums, after, split=False):
        chosen = [picks[i] for i in order[n]]
        gates = jnp.concatenate([shared["mine"][i : i + 1] for i in order[n]], axis=0)
        signs = jnp.concatenate([shared["signs"][i : i + 1] for i in order[n]], axis=0)
        head = list(sums) + [gates, signs, adapter_out, down_in_t]
        mid, cost = None, NO_COST
        if split:
            mid = run_middle(head, chosen, after)
            lines, after, cost = [mid.pop()], [mid[0]], LAST_COST
        dense, new, extra = run_back(
            share_start,
            share,
            head,
            mid,
            chunk_x[n],
            chunk_c[n],
            weights,
            adapter_in_t,
            down_out,
            chosen,
            totals,
            after,
            cost,
        )
        lines = lines if split else extra
        totals[:] = new
        for at, i in enumerate(order[n]):
            signed[i] = lines[0][at : at + 1]
            back[i] = dense[at] if i == 0 else hop(dense[at], i, experts)
        return [new[0]]

    chunks = len(order)
    units = [(n, j) for n in range(chunks) for j in range(3)]
    total = len(units)
    after = []
    if parts == 4 and per_chunk == 1:
        term, near, inner, far, carried, final = {}, {}, {}, {}, {}, {}
        for t in range(total + 3 * LAG):
            old = t - LAG
            pairs = {}
            if 0 <= t - LAG < total:
                pairs["b"] = (term[old], near[old])
            if 0 <= t - 2 * LAG < total:
                pairs["c"] = (inner[old], far[old])
            if 0 <= t - 3 * LAG < total:
                pairs["d"] = (carried[old], near[old])
            n, j = units[t] if t < total else (None, None)
            new, sums = step(n, j, pairs, after, logits=t == 4)
            if new is not None:
                term[t] = new
            if "c" in sums:
                carried[t] = sums["c"]
                way = (INWARD if new is not None else []) + OUTWARD
                near[t] = lax.ppermute(carried[t], "dp", way)
            elif new is not None:
                near[t] = lax.ppermute(new, "dp", INWARD)
            if "b" in sums:
                inner[t] = sums["b"]
                far[t] = lax.ppermute(inner[t], "dp", MIDDLE)
            after = [new if new is not None else list(sums.values())[0]]
            if "d" in sums:
                unit = t - 3 * LAG
                final[unit] = sums["d"]
                if unit % 3 == 2:
                    m = unit // 3
                    after = finish(m, [final[3 * m + f] for f in range(3)], after, m == chunks - 1)
    else:
        top = jnp.concatenate([tokens, cotangent], axis=1)
        low = jnp.pad(routes_pad, ((0, 0), (0, 2 * features - token_count)))
        spread_start(jnp.concatenate([top, low], axis=0))
        sums = {}
        for n, j in units:
            new = step(n, j, {}, after)[0]
            after = [new]
            sums[n, j] = lax.psum(new, "dp")
        step(None, None, {}, after, logits=True)
        for n in range(chunks):
            after = finish(n, [sums[n, j] for j in range(3)], after)

    gathered = gather_direct(jnp.concatenate([signed[i] for i in range(experts)], axis=0), experts)
    out_y, grad_tokens, grad_router = run_end(
        [back[i] for i in range(experts)], packs, gathered, shared["gates"], shared["routes"], router_t, after
    )
    grad_a, grad_b, grad_di, grad_do = totals
    if share % 128:
        grad_b = lax.dynamic_slice_in_dim(grad_b, z_index * share, share, 2)
        grad_di = lax.dynamic_slice_in_dim(grad_di, z_index * share, share, 1)
    return (
        out_y,
        grad_tokens,
        grad_router.T,
        jnp.swapaxes(grad_a, 1, 2)[None],
        grad_b[None],
        grad_di.T[None],
        grad_do[None],
    )


def solution(mesh):
    in_specs = (
        P(("groups", "expert"), "dp"),
        P(("groups", "expert"), None),
        P("dp", None),
        P("expert", "dp", None),
        P("expert", None, "dp", None),
        P("expert", None, "dp", None),
        P("expert", None, None, None),
        P("expert", None, None),
        P("expert", None, "dp"),
        P(("groups", "expert"), "dp"),
    )
    out_specs = (
        P(("groups", "expert"), "dp"),
        P(("groups", "expert"), "dp"),
        P(("groups", "dp"), None),
        P(("groups", "expert"), None, "dp", None),
        P(("groups", "expert"), None, None, "dp"),
        P(("groups", "expert"), "dp", None),
        P(("groups", "expert"), None, "dp"),
    )
    return jax.shard_map(shards, mesh=mesh, in_specs=in_specs, out_specs=out_specs, check_vma=False)
```

```python
import functools

import jax
import jax.numpy as jnp
import numpy as np
from jax import lax
from jax.experimental import pallas as pl
from jax.experimental.pallas import tpu as pltpu
from jax.sharding import PartitionSpec as P

NF4_LEVELS = (
    -1.0,
    -0.6961928009986877,
    -0.5250730514526367,
    -0.39491748809814453,
    -0.28444138169288635,
    -0.18477343022823334,
    -0.09105003625154495,
    0.0,
    0.07958029955625534,
    0.16093020141124725,
    0.24611230194568634,
    0.3379152424240112,
    0.44070982933044434,
    0.5626170039176941,
    0.7229568362236023,
    1.0,
)
SCALE = 0.5
BF16 = jnp.bfloat16
F32 = jnp.float32
LAG = 2
LAST_COST = pl.CostEstimate(flops=6 * 10**9, bytes_accessed=16 * 10**6, transcendentals=0)
NO_COST = pl.CostEstimate(flops=0, bytes_accessed=0, transcendentals=0)
INWARD = [(0, 1), (3, 2)]
MIDDLE = [(1, 2), (2, 1)]
OUTWARD = [(1, 0), (2, 3)]


def dot(left, right):
    return jnp.dot(left, right, preferred_element_type=F32)


def dot_tn(left, right):
    return lax.dot_general(left, right, (((0,), (0,)), ((), ())), preferred_element_type=F32)


def dot_nt(left, right):
    return lax.dot_general(left, right, (((1,), (1,)), ((), ())), preferred_element_type=F32)


def dequantize_kernel(code_ref, scale_ref, level_ref, spread_ref, *refs, field):
    out_ref = refs[-1]
    rows, width = code_ref.shape
    step = 64
    table = jnp.broadcast_to(level_ref[0:1, :], (step, 128))
    scales = scale_ref[0]
    high = scales.astype(BF16)
    rest = scales - high.astype(F32)
    middle = rest.astype(BF16)
    low = (rest - middle.astype(F32)).astype(BF16)
    for column in range(0, width, 128):
        spread = spread_ref[:, column : column + 128]
        wide = (dot_tn(high, spread) + dot_tn(middle, spread)) + dot_tn(low, spread)
        for row in range(0, rows, step):
            code = (code_ref[row : row + step, column : column + 128] >> (4 * field)) & 15
            level = jnp.take_along_axis(table, code, axis=1)
            out_ref[row : row + step, column : column + 128] = (
                level * wide[row : row + step]
            ).astype(BF16)


def dequantize(codes, scales, levels, spread, field, *after):
    features, width = codes.shape
    blocks = scales.shape[1]
    rows = min(256, features)
    return pl.pallas_call(
        functools.partial(dequantize_kernel, field=field),
        grid=(features // rows,),
        in_specs=[
            pl.BlockSpec((rows, width), lambda i: (i, 0)),
            pl.BlockSpec((1, blocks, rows), lambda i: (field, 0, i)),
            pl.BlockSpec((8, 128), lambda i: (0, 0)),
            pl.BlockSpec((blocks, width), lambda i: (0, 0)),
        ]
        + [pl.BlockSpec(memory_space=pl.ANY)] * len(after),
        out_specs=pl.BlockSpec((rows, width), lambda i: (i, 0)),
        out_shape=jax.ShapeDtypeStruct((features, width), BF16),
        compiler_params=pltpu.CompilerParams(vmem_limit_bytes=(12 if after else 56) * 2**20),
        cost_estimate=NO_COST,
    )(codes, scales, levels, spread, *after)


def call(body, args, after, shapes, piped=False):
    smem = pl.BlockSpec(memory_space=pltpu.SMEM)
    count = len(args)
    extra = len(after)

    def whole(shape):
        if piped:
            return pl.BlockSpec(shape, lambda i: (0,) * len(shape))
        return pl.BlockSpec(memory_space=pltpu.VMEM)

    def kernel(*refs):
        body(list(refs[:count]), list(refs[count + extra :]))

    out = pl.pallas_call(
        kernel,
        grid=(1,) if piped else (),
        in_specs=[smem if a.dtype == jnp.int32 else whole(a.shape) for a in args]
        + [pl.BlockSpec(memory_space=pl.ANY)] * extra,
        out_specs=[whole(shape) for shape, _ in shapes],
        out_shape=[jax.ShapeDtypeStruct(shape, dtype) for shape, dtype in shapes],
        compiler_params=pltpu.CompilerParams(vmem_limit_bytes=(24 if piped else 10) * 2**20),
        cost_estimate=NO_COST,
    )(*args, *after)
    return list(out)


def run_step(end, kind, unit, pairs, pack, logits_of, after):
    args, shapes, count = [end], [], 0
    if kind is not None:
        rows, blocks, weight, low = unit
        if kind == 1:
            args.append(rows)
            count = rows.shape[0]
        else:
            features = weight.shape[0]
            count = sum(pick.shape[0] for pick, _, _ in blocks)
            for pick, block, _ in blocks:
                args += [pick, block]
            shapes.append(((count, features), BF16))
        args += [weight, low]
        shapes.append(((count, weight.shape[1] + low.shape[-2]), BF16))
    for name in pairs:
        args += list(pairs[name])
        shapes.append((pairs[name][0].shape, pairs[name][0].dtype))
    if pack is not None:
        args += list(pack)
        tokens, _, routes = pack
        shapes.append(((tokens.shape[0] + routes.shape[0], 2 * tokens.shape[1]), BF16))
    if logits_of is not None:
        router, packs = logits_of
        token_count = packs[0].shape[0] - 16
        args += [router] + packs
        shapes.append(((router.shape[0], token_count * len(packs)), F32))

    def body(ins, outs):
        is_end = ins.pop(0)[0]
        term = None
        if kind is not None:
            if kind == 1:
                rows_ref = ins.pop(0)
            else:
                rows_ref = outs.pop(0)
                found = []
                for pick, block, at in blocks:
                    pick_ref, block_ref = ins.pop(0), ins.pop(0)
                    found.append(
                        dot(pick_ref[...], block_ref[: pick.shape[1], at : at + rows_ref.shape[1]])
                    )
                rows_ref[...] = (jnp.concatenate(found, axis=0) if len(found) > 1 else found[0]).astype(
                    BF16
                )
            weight_ref, low_ref = ins.pop(0), ins.pop(0)
            term = outs.pop(0)
            width = weight_ref.shape[1]
            for column in range(0, width, 512):
                tile = slice(column, column + 512)
                term[:, tile] = dot(rows_ref[...], weight_ref[:, tile]).astype(BF16)
            low_map = low_ref[...] if kind == 2 else low_ref[kind]
            term[:, width:] = dot_nt(rows_ref[...], low_map).astype(BF16)
        for name in pairs:
            left, right, out = ins.pop(0), ins.pop(0), outs.pop(0)
            if name in "be" or (name == "c" and term is None):
                out[...] = (left[...].astype(F32) + right[...].astype(F32)).astype(out.dtype)
            elif name == "c":

                @pl.when(is_end == 1)
                def _(out=out):
                    out[...] = term[...]

                @pl.when(is_end == 0)
                def _(out=out, left=left, right=right):
                    out[...] = (left[...].astype(F32) + right[...].astype(F32)).astype(BF16)

            else:

                @pl.when(is_end == 1)
                def _(out=out, right=right):
                    out[...] = right[...]

                @pl.when(is_end == 0)
                def _(out=out, left=left):
                    out[...] = left[...]

        if pack is not None:
            tokens_ref, cots_ref, routes_ref, out = ins.pop(0), ins.pop(0), ins.pop(0), outs.pop(0)
            top, left = tokens_ref.shape
            out[:top, :left] = tokens_ref[...]
            out[:top, left:] = cots_ref[...]
            out[top:, : routes_ref.shape[1]] = routes_ref[...]
        if logits_of is not None:
            router_ref, out = ins.pop(0), outs.pop(0)
            features = router_ref.shape[1]
            for number in range(len(packs)):
                block = ins.pop(0)
                out[:, number * token_count : (number + 1) * token_count] = dot_nt(
                    router_ref[...], block[:token_count, :features]
                )

    return call(body, args, after, shapes)


def middle_shapes(rows, hidden_width, rank, sources, tokens):
    wide, low = ((rows, hidden_width), BF16), ((rows, rank), BF16)
    return [wide, wide, wide] + [low] * 7 + [((rows, 1), F32), ((sources, tokens), F32)]


def middle_body(ins, outs):
    gate_ref, up_ref, cot_ref, gates_ref, signs_ref, maps, down_ref = ins[:7]
    picks_ref = ins[7:]
    sources = len(picks_ref)
    rows = gate_ref.shape[0]
    cap = rows // sources
    hidden_width = maps.shape[2]
    hidden_ref, grad_gate_ref, grad_up_ref, hl_ref, lg_ref, lu_ref, hlg_ref, clg_ref = outs[:8]
    ag_ref, au_ref, gate_out, signed_ref = outs[8:]
    ag_ref[...] = gate_ref[:, hidden_width:]
    au_ref[...] = up_ref[:, hidden_width:]
    chosen = [pick[...].astype(F32) for pick in picks_ref]
    gate = [jnp.sum(chosen[i] * gates_ref[i : i + 1, :], axis=1, keepdims=True) for i in range(sources)]
    gate = jnp.concatenate(gate, axis=0) if sources > 1 else gate[0]
    gate_out[...] = gate
    cot_low = cot_ref[:, hidden_width:]
    total = jnp.zeros((rows, 1), F32)
    step = 512
    for column in range(0, hidden_width, step):
        tile = slice(column, column + step)
        g = gate_ref[:, tile].astype(F32) + SCALE * dot(gate_ref[:, hidden_width:], maps[0, :, tile])
        u = up_ref[:, tile].astype(F32) + SCALE * dot(up_ref[:, hidden_width:], maps[1, :, tile])
        h = cot_ref[:, tile].astype(F32) + SCALE * dot(cot_low, down_ref[:, tile])
        sigma = jax.nn.sigmoid(g)
        silu = g * sigma
        hidden = (silu * u).astype(BF16)
        total = total + jnp.sum(hidden.astype(F32) * h, axis=1, keepdims=True)
        h = h * gate
        hidden_ref[:, tile] = hidden
        grad_gate_ref[:, tile] = (h * u * sigma * (1.0 + g * (1.0 - sigma))).astype(BF16)
        grad_up_ref[:, tile] = (h * silu).astype(BF16)
    hidden_low = dot_nt(hidden_ref[...], down_ref[...]).astype(BF16)
    hl_ref[...] = hidden_low
    hlg_ref[...] = (hidden_low.astype(F32) * gate).astype(BF16)
    clg_ref[...] = (cot_low.astype(F32) * gate).astype(BF16)
    lg_ref[...] = dot_nt(grad_gate_ref[...], maps[0]).astype(BF16)
    lu_ref[...] = dot_nt(grad_up_ref[...], maps[1]).astype(BF16)
    for i in range(sources):
        line = jnp.sum(chosen[i] * total[i * cap : (i + 1) * cap], axis=0, keepdims=True)
        signed_ref[i : i + 1, :] = line * signs_ref[i : i + 1, :]


def run_middle(head, picks, after):
    rows, maps = head[0].shape[0], head[5]
    shapes = middle_shapes(rows, maps.shape[2], maps.shape[1], len(picks), picks[0].shape[1])
    return call(middle_body, head + picks, after, shapes)


def run_back(share_start, share, head, mid, rows_x, rows_c, weights, adapter_in_t, down_out, picks, totals, after, cost):
    rows, hidden_width = rows_x.shape[0], weights[0].shape[1]
    rank, features = down_out.shape
    sources = len(picks)
    cap = rows // sources
    width = hidden_width if share % 128 else share
    tile = min(256, features)
    tokens = picks[0].shape[1]

    def fixed(value):
        return pl.BlockSpec(value.shape, lambda i, n=value.ndim: (0,) * n)

    last = pl.BlockSpec((rows, tile), lambda i: (0, i))
    low = pl.BlockSpec((rank, tile), lambda i: (0, i))
    pair = pl.BlockSpec((2, rank, tile), lambda i: (0, 0, i))
    total_specs = [
        pair,
        pl.BlockSpec((2, rank, width), lambda i: (0, 0, 0)),
        pl.BlockSpec((rank, width), lambda i: (0, 0)),
        low,
    ]
    fused = mid is None
    lead = head if fused else list(mid)
    inner = middle_shapes(rows, hidden_width, rank, sources, tokens)
    args = [share_start] + lead + [rows_x, rows_c] + list(weights) + [adapter_in_t, down_out]
    args += picks + totals + after
    specs = [pl.BlockSpec(memory_space=pltpu.SMEM)] + [fixed(value) for value in lead]
    resident = pl.BlockSpec(memory_space=pltpu.VMEM)
    specs += [last, last, resident, resident, resident, pair, low] + [fixed(pick) for pick in picks]
    specs += total_specs[: len(totals)] + [pl.BlockSpec(memory_space=pl.ANY)] * len(after)
    shapes = [((2, tokens, features), BF16)] * sources
    shapes += [((2, rank, features), F32), ((2, rank, width), F32), ((rank, width), F32), ((rank, features), F32)]
    out_specs = [pl.BlockSpec((2, tokens, tile), lambda i: (0, 0, i))] * sources + total_specs
    if fused:
        shapes.append(inner[-1])
        out_specs.append(pl.BlockSpec(inner[-1][0], lambda i: (0, 0)))
    given = len(totals)
    led = 1 + len(lead)

    def body(*refs):
        start = pl.multiple_of(refs[0][0], 128) if share % 128 == 0 else 0
        x_ref, c_ref, wg, wu, wd, maps, down_ref = refs[led : led + 7]
        picks_ref = refs[led + 7 : led + 7 + sources]
        old = refs[led + 7 + sources : led + 7 + sources + given]
        outs = refs[len(args) :]
        backs, new = outs[:sources], outs[sources : sources + 4]
        middle = refs[1:led]
        if fused:
            middle = outs[sources + 5 :]

            @pl.when(pl.program_id(0) == 0)
            def _():
                middle_body(list(refs[1:led]) + list(picks_ref), list(middle) + [outs[sources + 4]])

        h_ref, gg_ref, gu_ref, hl_ref, lg_ref, lu_ref, hlg_ref, clg_ref, ag_ref, au_ref, gate_ref = middle
        lines = pl.ds(pl.multiple_of(pl.program_id(0) * tile, tile), tile)
        out = dot_nt(h_ref[...], wd[lines, :]) + SCALE * dot(hl_ref[...], down_ref[...])
        slot = (dot_nt(gg_ref[...], wg[lines, :]) + dot_nt(gu_ref[...], wu[lines, :])) + SCALE * (
            dot(lg_ref[...], maps[0]) + dot(lu_ref[...], maps[1])
        )
        for which, value in enumerate((out * gate_ref[...], slot)):
            for i in range(sources):
                part = value[i * cap : (i + 1) * cap].astype(BF16)
                backs[i][which] = dot_tn(picks_ref[i][...], part).astype(BF16)

        def add(which, index, value):
            value = SCALE * value
            if given:
                value = value + old[which][index]
            new[which][index] = value

        add(0, 0, dot_tn(lg_ref[...], x_ref[...]))
        add(0, 1, dot_tn(lu_ref[...], x_ref[...]))
        add(3, ..., dot_tn(hlg_ref[...], c_ref[...]))

        @pl.when(pl.program_id(0) == 0)
        def _():
            columns = pl.ds(start, width)
            add(1, 0, dot_tn(ag_ref[...], gg_ref[:, columns]))
            add(1, 1, dot_tn(au_ref[...], gu_ref[:, columns]))
            add(2, ..., dot_tn(clg_ref[...], h_ref[:, columns]))

    out = pl.pallas_call(
        body,
        grid=(features // tile,),
        in_specs=specs,
        out_specs=out_specs,
        out_shape=[jax.ShapeDtypeStruct(shape, dtype) for shape, dtype in shapes],
        scratch_shapes=[pltpu.VMEM(shape, dtype) for shape, dtype in inner[:-1]] if fused else [],
        compiler_params=pltpu.CompilerParams(vmem_limit_bytes=20 * 2**20),
        cost_estimate=cost,
    )(*args)
    return list(out[:sources]), list(out[sources : sources + 4]), list(out[sources + 4 :])


def run_end(backs, packs, gathered, gates, routes, router_t, after):
    token_count = backs[0].shape[1]
    experts, features = router_t.shape
    args = backs + packs + gathered + [gates, routes, router_t]
    shapes = [((token_count, features), BF16), ((token_count, features), BF16), ((experts, features), F32)]

    def body(ins, outs):
        backs_ref, packs_ref, gathered_ref = ins[:experts], ins[experts : 2 * experts], ins[2 * experts : 3 * experts]
        gates_ref, routes_ref, router_ref = ins[3 * experts :]
        number = lax.broadcasted_iota(jnp.int32, (experts, 1), 0).astype(F32)
        terms, first_line = [], None
        for i in range(experts):
            at = slice(i * token_count, (i + 1) * token_count)
            margin = sum_tree([gathered_ref[j][i ^ j : (i ^ j) + 1, :] for j in range(experts)])
            step = gates_ref[0:1, at] * gates_ref[1:2, at] * margin
            line = step * (
                (routes_ref[0:1, at] == number).astype(F32) - (routes_ref[1:2, at] == number).astype(F32)
            )
            line = line.astype(BF16)
            first_line = line if i == 0 else first_line
            terms.append(dot(line, packs_ref[i][:token_count, :features]))
        outs[2][...] = sum_tree(terms)
        outs[0][...] = sum_tree([back[0].astype(F32) for back in backs_ref]).astype(BF16)
        outs[1][...] = (
            sum_tree([back[1].astype(F32) for back in backs_ref])
            + dot_tn(first_line, router_ref[...])
        ).astype(BF16)

    return call(body, args, after, shapes, True)


def hop(value, step, count):
    return lax.ppermute(value, "expert", [(e, e ^ step) for e in range(count)])


def gather_direct(value, count):
    return [value] + [hop(value, step, count) for step in range(1, count)]


def gather_sources(value, count):
    got = [value] + [None] * (count - 1)
    bits = [1 << b for b in range(count.bit_length() - 1)]
    for index in sorted(range(1, count), key=lambda i: bin(i).count("1")):
        low_bit = index & -index
        got[index] = hop(got[index ^ low_bit], low_bit, count)
    return got


def sum_tree(values):
    while len(values) > 1:
        values = [values[2 * i] + values[2 * i + 1] for i in range(len(values) // 2)]
    return values[0]


def sum_dp(value, parts):
    if parts & (parts - 1):
        return lax.psum(value, "dp")
    step = 1
    while step < parts:
        value = value + lax.ppermute(value, "dp", [(z, z ^ step) for z in range(parts)])
        step *= 2
    return value


def shards(
    tokens,
    routes,
    router_w,
    codes,
    scales,
    adapter_in,
    adapter_out,
    down_in,
    down_out,
    cotangent,
):
    token_count, features = tokens.shape
    slots = routes.shape[1]
    experts = router_w.shape[1]
    capacity = 3 * token_count * slots // (2 * experts)
    codes, scales_t = codes[0], jnp.swapaxes(scales[0], 1, 2)
    adapter_in_t = jnp.swapaxes(adapter_in[0], 1, 2)
    adapter_out, down_out = adapter_out[0], down_out[0]
    down_in_t = down_in[0].T
    router_t = router_w.T
    hidden_width = codes.shape[1]
    blocks = scales_t.shape[1]
    parts = lax.axis_size("dp")
    me = lax.axis_index("expert").astype(F32)
    z_index = lax.axis_index("dp")
    share = hidden_width // parts
    share_start = (z_index * share).astype(jnp.int32).reshape(1)
    end = ((z_index == 0) | (z_index == parts - 1)).astype(jnp.int32).reshape(1)
    number = lax.broadcasted_iota(jnp.int32, (experts, 1), 0).astype(F32)

    table = np.zeros((8, 128), np.float32)
    table[:, :16] = np.asarray(NF4_LEVELS, np.float32)
    levels = jnp.asarray(table)
    block_of = np.arange(hidden_width) // (hidden_width // blocks)
    spread = jnp.asarray(np.arange(blocks)[:, None] == block_of[None, :], BF16)
    before = jnp.asarray(np.arange(token_count)[:, None] < np.arange(token_count)[None, :], BF16)
    row_number = jnp.asarray(np.arange(capacity)[:, None], F32)
    weights = [dequantize(codes, scales_t, levels, spread, 0), None, None]

    per_chunk = max(1, experts // 4)
    order = [list(range(i, i + per_chunk)) for i in range(0, experts, per_chunk)]
    if len(order) == 4:
        order = [order[0], order[2], order[3], order[1]]

    def picks_of(first, second):
        mine = (first == me) | (second == me)
        pad = jnp.concatenate([mine, mine, mine, mine, mine, mine, mine, mine], axis=0)
        place = dot(pad[: max(8, mine.shape[0])].astype(BF16), before)
        return [
            (mine[i : i + 1] & (place[i : i + 1] == row_number)).astype(BF16) for i in range(mine.shape[0])
        ]

    routes_t = routes.T.astype(F32)
    picks = picks_of(routes_t[0:1], routes_t[1:2])
    routes_pad = jnp.pad(routes_t.astype(BF16), ((0, 14), (0, 0)))
    packs, chunk_x, chunk_c, shared = [], {}, {}, {}

    def spread_start(packed):
        packs[:] = gather_sources(packed, experts)
        rows = [pack[token_count : token_count + 2, :token_count].astype(F32) for pack in packs]
        shared["routes"] = jnp.concatenate(rows, axis=1)
        if experts > 1:
            first = jnp.concatenate([row[0:1] for row in rows[1:]], axis=0)
            second = jnp.concatenate([row[1:2] for row in rows[1:]], axis=0)
            picks[1:] = picks_of(first, second)

    def settle_gates(logits, more, after):
        first = (shared["routes"][0:1] == me).astype(F32)
        args = [logits] + ([more] if more is not None else []) + [shared["routes"], first]
        row = ((1, first.shape[1]), F32)

        def body(ins, outs):
            total = ins[0][...] + (ins[1][...] if more is not None else 0.0)
            routes_ref, first_ref = ins[-2:]
            which = lax.broadcasted_iota(jnp.int32, (experts, 1), 0).astype(F32)
            chosen = [
                jnp.sum(jnp.where(routes_ref[k : k + 1, :] == which, total, 0.0), axis=0, keepdims=True)
                for k in range(2)
            ]
            margin = chosen[0] - chosen[1]
            gate, other = jax.nn.sigmoid(margin), jax.nn.sigmoid(-margin)
            outs[0][0:1, :] = gate
            outs[0][1:2, :] = other
            mine = first_ref[...] > 0.5
            outs[1][...] = jnp.where(mine, gate, other)
            outs[2][...] = jnp.where(mine, 1.0, -1.0)

        out = call(body, args, after, [((2, first.shape[1]), F32), row, row])
        shared["gates"] = out[0]
        shared["mine"] = out[1].reshape(experts, token_count)
        shared["signs"] = out[2].reshape(experts, token_count)

    def step(n, j, pairs, after, logits=False):
        kind, unit, pack = None, None, None
        if n is not None:
            kind = j
            if weights[j] is None:
                weights[j] = dequantize(codes, scales_t, levels, spread, j, *after)
            if j == 0:
                taken = [(picks[i], packs[i] if packs else tokens, 0) for i in order[n]]
                unit = (None, taken, weights[0], adapter_in_t)
            elif j == 1:
                unit = (chunk_x[n], None, weights[1], adapter_in_t)
            else:
                unit = (None, [(picks[i], packs[i], features) for i in order[n]], weights[2], down_out)
            if j == 0 and not packs:
                pack = (tokens, cotangent, routes_pad)
        logits_of = (router_t, packs) if logits else None
        out = run_step(end, kind, unit, pairs, pack, logits_of, after)
        if logits:
            shared["logits"] = out.pop()
        if pack is not None:
            spread_start(out.pop())
        term = None
        if kind is not None:
            if kind == 0:
                chunk_x[n] = out.pop(0)
            elif kind == 2:
                chunk_c[n] = out.pop(0)
            term = out.pop(0)
        return term, dict(zip(pairs, out))

    back, totals, signed, waiting = {}, [], {}, {}

    def finish(n, sums, after, split=False):
        chosen = [picks[i] for i in order[n]]
        gates = jnp.concatenate([shared["mine"][i : i + 1] for i in order[n]], axis=0)
        signs = jnp.concatenate([shared["signs"][i : i + 1] for i in order[n]], axis=0)
        head = list(sums) + [gates, signs, adapter_out, down_in_t]
        mid, cost = None, NO_COST
        if split:
            mid = run_middle(head, chosen, after)
            lines, after, cost = [mid.pop()], [mid[0]], LAST_COST
        dense, new, extra = run_back(
            share_start,
            share,
            head,
            mid,
            chunk_x[n],
            chunk_c[n],
            weights,
            adapter_in_t,
            down_out,
            chosen,
            totals,
            after,
            cost,
        )
        lines = lines if split else extra
        totals[:] = new
        for at, i in enumerate(order[n]):
            signed[i] = lines[0][at : at + 1]
            waiting[i] = dense[at]
        return [new[0]]

    def send_back(n):
        for i in order[n]:
            value = waiting[i]
            if i:
                value = hop(value, i, experts)
            back[i] = value

    chunks = len(order)
    units = [(n, j) for n in range(chunks) for j in range(3)]
    total = len(units)
    after = []
    if parts == 4 and per_chunk == 1:
        term, near, inner, far, carried, final = {}, {}, {}, {}, {}, {}
        for t in range(total + 3 * LAG):
            old = t - LAG
            pairs = {}
            if 0 <= t - LAG < total:
                pairs["b"] = (term[old], near[old])
            if 0 <= t - 2 * LAG < total:
                pairs["c"] = (inner[old], far[old])
            if 0 <= t - 3 * LAG < total:
                pairs["d"] = (carried[old], near[old])
            n, j = units[t] if t < total else (None, None)
            if t == 8:
                pairs["e"] = (shared["logits"], nearby)
            new, sums = step(n, j, pairs, after, logits=t == 6)
            if t == 6:
                nearby = lax.ppermute(shared["logits"], "dp", [(z, z ^ 1) for z in range(4)])
            if t == 8:
                shared["logits"] = sums.pop("e")
                distant = lax.ppermute(shared["logits"], "dp", [(z, z ^ 2) for z in range(4)])
            if new is not None:
                term[t] = new
            if "c" in sums:
                carried[t] = sums["c"]
                way = (INWARD if new is not None else []) + OUTWARD
                near[t] = lax.ppermute(carried[t], "dp", way)
            elif new is not None:
                near[t] = lax.ppermute(new, "dp", INWARD)
            if "b" in sums:
                inner[t] = sums["b"]
                far[t] = lax.ppermute(inner[t], "dp", MIDDLE)
            after = [new if new is not None else list(sums.values())[0]]
            if "d" in sums:
                final[t - 3 * LAG] = sums["d"]
            for m in range(chunks):
                wait = 2 if m < chunks - 2 else (1 if m < chunks - 1 else 0)
                if t == 3 * m + 2 + 3 * LAG + wait:
                    if m == 0:
                        settle_gates(shared["logits"], distant, after)
                    last = m == chunks - 1
                    after = finish(m, [final[3 * m + f] for f in range(3)], after, last)
                    send_back(m)
    else:
        top = jnp.concatenate([tokens, cotangent], axis=1)
        low = jnp.pad(routes_pad, ((0, 0), (0, 2 * features - token_count)))
        spread_start(jnp.concatenate([top, low], axis=0))
        sums = {}
        for n, j in units:
            new = step(n, j, {}, after)[0]
            after = [new]
            sums[n, j] = lax.psum(new, "dp")
        step(None, None, {}, after, logits=True)
        settle_gates(sum_dp(shared["logits"], parts), None, [])
        for n in range(chunks):
            after = finish(n, [sums[n, j] for j in range(3)], after)
            send_back(n)

    gathered = gather_direct(jnp.concatenate([signed[i] for i in range(experts)], axis=0), experts)
    out_y, grad_tokens, grad_router = run_end(
        [back[i] for i in range(experts)], packs, gathered, shared["gates"], shared["routes"], router_t, after
    )
    grad_a, grad_b, grad_di, grad_do = totals
    if share % 128:
        grad_b = lax.dynamic_slice_in_dim(grad_b, z_index * share, share, 2)
        grad_di = lax.dynamic_slice_in_dim(grad_di, z_index * share, share, 1)
    return (
        out_y,
        grad_tokens,
        grad_router.T,
        jnp.swapaxes(grad_a, 1, 2)[None],
        grad_b[None],
        grad_di.T[None],
        grad_do[None],
    )


def solution(mesh):
    in_specs = (
        P(("groups", "expert"), "dp"),
        P(("groups", "expert"), None),
        P("dp", None),
        P("expert", "dp", None),
        P("expert", None, "dp", None),
        P("expert", None, "dp", None),
        P("expert", None, None, None),
        P("expert", None, None),
        P("expert", None, "dp"),
        P(("groups", "expert"), "dp"),
    )
    out_specs = (
        P(("groups", "expert"), "dp"),
        P(("groups", "expert"), "dp"),
        P(("groups", "dp"), None),
        P(("groups", "expert"), None, "dp", None),
        P(("groups", "expert"), None, None, "dp"),
        P(("groups", "expert"), "dp", None),
        P(("groups", "expert"), None, "dp"),
    )
    return jax.shard_map(shards, mesh=mesh, in_specs=in_specs, out_specs=out_specs, check_vma=False)
```

```python
import functools

import jax
import jax.numpy as jnp
import numpy as np
from jax import lax
from jax.experimental import pallas as pl
from jax.experimental.pallas import tpu as pltpu
from jax.sharding import PartitionSpec as P

NF4_LEVELS = (
    -1.0,
    -0.6961928009986877,
    -0.5250730514526367,
    -0.39491748809814453,
    -0.28444138169288635,
    -0.18477343022823334,
    -0.09105003625154495,
    0.0,
    0.07958029955625534,
    0.16093020141124725,
    0.24611230194568634,
    0.3379152424240112,
    0.44070982933044434,
    0.5626170039176941,
    0.7229568362236023,
    1.0,
)
SCALE = 0.5
BF16 = jnp.bfloat16
F32 = jnp.float32
LAG = 2
LAST_COST = pl.CostEstimate(flops=6 * 10**9, bytes_accessed=16 * 10**6, transcendentals=0)
NO_COST = pl.CostEstimate(flops=0, bytes_accessed=0, transcendentals=0)
INWARD = [(0, 1), (3, 2)]
MIDDLE = [(1, 2), (2, 1)]
OUTWARD = [(1, 0), (2, 3)]


def dot(left, right):
    return jnp.dot(left, right, preferred_element_type=F32)


def dot_tn(left, right):
    return lax.dot_general(left, right, (((0,), (0,)), ((), ())), preferred_element_type=F32)


def dot_nt(left, right):
    return lax.dot_general(left, right, (((1,), (1,)), ((), ())), preferred_element_type=F32)


def select_level(code):
    found = list(NF4_LEVELS)
    for bit in range(4):
        odd = (code & (1 << bit)) != 0
        found = [jnp.where(odd, found[2 * i + 1], found[2 * i]) for i in range(len(found) // 2)]
    return found[0]


def dequantize_kernel(code_ref, scale_ref, level_ref, spread_ref, *refs, field):
    out_ref = refs[-1]
    rows, width = code_ref.shape
    step = 64
    table = jnp.broadcast_to(level_ref[0:1, :], (step, 128))
    scales = scale_ref[0]
    high = scales.astype(BF16)
    rest = scales - high.astype(F32)
    middle = rest.astype(BF16)
    low = (rest - middle.astype(F32)).astype(BF16)
    for column in range(0, width, 128):
        spread = spread_ref[:, column : column + 128]
        wide = (dot_tn(high, spread) + dot_tn(middle, spread)) + dot_tn(low, spread)
        for row in range(0, rows, step):
            code = (code_ref[row : row + step, column : column + 128] >> (4 * field)) & 15
            if column // 128 % 3 == 1:
                level = select_level(code)
            else:
                level = jnp.take_along_axis(table, code, axis=1)
            out_ref[row : row + step, column : column + 128] = (
                level * wide[row : row + step]
            ).astype(BF16)


def dequantize(codes, scales, levels, spread, field, *after):
    features, width = codes.shape
    blocks = scales.shape[1]
    rows = min(256, features)
    return pl.pallas_call(
        functools.partial(dequantize_kernel, field=field),
        grid=(features // rows,),
        in_specs=[
            pl.BlockSpec((rows, width), lambda i: (i, 0)),
            pl.BlockSpec((1, blocks, rows), lambda i: (field, 0, i)),
            pl.BlockSpec((8, 128), lambda i: (0, 0)),
            pl.BlockSpec((blocks, width), lambda i: (0, 0)),
        ]
        + [pl.BlockSpec(memory_space=pl.ANY)] * len(after),
        out_specs=pl.BlockSpec((rows, width), lambda i: (i, 0)),
        out_shape=jax.ShapeDtypeStruct((features, width), BF16),
        compiler_params=pltpu.CompilerParams(vmem_limit_bytes=(12 if after else 56) * 2**20),
        cost_estimate=NO_COST,
    )(codes, scales, levels, spread, *after)


def call(body, args, after, shapes, piped=False, limit=24):
    smem = pl.BlockSpec(memory_space=pltpu.SMEM)
    count = len(args)
    extra = len(after)

    def whole(shape):
        if piped:
            return pl.BlockSpec(shape, lambda i: (0,) * len(shape))
        return pl.BlockSpec(memory_space=pltpu.VMEM)

    def kernel(*refs):
        body(list(refs[:count]), list(refs[count + extra :]))

    out = pl.pallas_call(
        kernel,
        grid=(1,) if piped else (),
        in_specs=[smem if a.dtype == jnp.int32 else whole(a.shape) for a in args]
        + [pl.BlockSpec(memory_space=pl.ANY)] * extra,
        out_specs=[whole(shape) for shape, _ in shapes],
        out_shape=[jax.ShapeDtypeStruct(shape, dtype) for shape, dtype in shapes],
        compiler_params=pltpu.CompilerParams(vmem_limit_bytes=(limit if piped else 10) * 2**20),
        cost_estimate=NO_COST,
    )(*args, *after)
    return list(out)


def run_step(end, kind, unit, pairs, pack, logits_of, after):
    args, shapes, count = [end], [], 0
    if kind is not None:
        rows, blocks, weight, low = unit
        if kind == 1:
            args.append(rows)
            count = rows.shape[0]
        else:
            features = weight.shape[0]
            count = sum(pick.shape[0] for pick, _, _ in blocks)
            for pick, block, _ in blocks:
                args += [pick, block]
            shapes.append(((count, features), BF16))
        args += [weight, low]
        shapes.append(((count, weight.shape[1] + low.shape[-2]), BF16))
    for name in pairs:
        args += list(pairs[name])
        shapes.append((pairs[name][0].shape, pairs[name][0].dtype))
    if pack is not None:
        args += list(pack)
        tokens, _, routes = pack
        shapes.append(((tokens.shape[0] + routes.shape[0], 2 * tokens.shape[1]), BF16))
    if logits_of is not None:
        router, packs = logits_of
        token_count = packs[0].shape[0] - 16
        args += [router] + packs
        shapes.append(((router.shape[0], token_count * len(packs)), F32))

    def body(ins, outs):
        is_end = ins.pop(0)[0]
        term = None
        if kind is not None:
            if kind == 1:
                rows_ref = ins.pop(0)
            else:
                rows_ref = outs.pop(0)
                found = []
                for pick, block, at in blocks:
                    pick_ref, block_ref = ins.pop(0), ins.pop(0)
                    found.append(
                        dot(pick_ref[...], block_ref[: pick.shape[1], at : at + rows_ref.shape[1]])
                    )
                rows_ref[...] = (jnp.concatenate(found, axis=0) if len(found) > 1 else found[0]).astype(
                    BF16
                )
            weight_ref, low_ref = ins.pop(0), ins.pop(0)
            term = outs.pop(0)
            width = weight_ref.shape[1]
            for column in range(0, width, 512):
                tile = slice(column, column + 512)
                term[:, tile] = dot(rows_ref[...], weight_ref[:, tile]).astype(BF16)
            low_map = low_ref[...] if kind == 2 else low_ref[kind]
            term[:, width:] = dot_nt(rows_ref[...], low_map).astype(BF16)
        for name in pairs:
            left, right, out = ins.pop(0), ins.pop(0), outs.pop(0)
            if name in "be" or (name == "c" and term is None):
                out[...] = (left[...].astype(F32) + right[...].astype(F32)).astype(out.dtype)
            elif name == "c":

                @pl.when(is_end == 1)
                def _(out=out):
                    out[...] = term[...]

                @pl.when(is_end == 0)
                def _(out=out, left=left, right=right):
                    out[...] = (left[...].astype(F32) + right[...].astype(F32)).astype(BF16)

            else:

                @pl.when(is_end == 1)
                def _(out=out, right=right):
                    out[...] = right[...]

                @pl.when(is_end == 0)
                def _(out=out, left=left):
                    out[...] = left[...]

        if pack is not None:
            tokens_ref, cots_ref, routes_ref, out = ins.pop(0), ins.pop(0), ins.pop(0), outs.pop(0)
            top, left = tokens_ref.shape
            out[:top, :left] = tokens_ref[...]
            out[:top, left:] = cots_ref[...]
            out[top:, : routes_ref.shape[1]] = routes_ref[...]
        if logits_of is not None:
            router_ref, out = ins.pop(0), outs.pop(0)
            features = router_ref.shape[1]
            for number in range(len(packs)):
                block = ins.pop(0)
                out[:, number * token_count : (number + 1) * token_count] = dot_nt(
                    router_ref[...], block[:token_count, :features]
                )

    return call(body, args, after, shapes)


def middle_shapes(rows, hidden_width, rank, sources, tokens):
    wide, low = ((rows, hidden_width), BF16), ((rows, rank), BF16)
    return [wide, wide, wide] + [low] * 7 + [((rows, 1), F32), ((sources, tokens), F32)]


def middle_body(ins, outs):
    gate_ref, up_ref, cot_ref, gates_ref, signs_ref, maps, down_ref = ins[:7]
    picks_ref = ins[7:]
    sources = len(picks_ref)
    rows = gate_ref.shape[0]
    cap = rows // sources
    hidden_width = maps.shape[2]
    hidden_ref, grad_gate_ref, grad_up_ref, hl_ref, lg_ref, lu_ref, hlg_ref, clg_ref = outs[:8]
    ag_ref, au_ref, gate_out, signed_ref = outs[8:]
    ag_ref[...] = gate_ref[:, hidden_width:]
    au_ref[...] = up_ref[:, hidden_width:]
    chosen = [pick[...].astype(F32) for pick in picks_ref]
    gate = [jnp.sum(chosen[i] * gates_ref[i : i + 1, :], axis=1, keepdims=True) for i in range(sources)]
    gate = jnp.concatenate(gate, axis=0) if sources > 1 else gate[0]
    gate_out[...] = gate
    cot_low = cot_ref[:, hidden_width:]
    total = jnp.zeros((rows, 1), F32)
    step = 512
    for column in range(0, hidden_width, step):
        tile = slice(column, column + step)
        g = gate_ref[:, tile].astype(F32) + SCALE * dot(gate_ref[:, hidden_width:], maps[0, :, tile])
        u = up_ref[:, tile].astype(F32) + SCALE * dot(up_ref[:, hidden_width:], maps[1, :, tile])
        h = cot_ref[:, tile].astype(F32) + SCALE * dot(cot_low, down_ref[:, tile])
        sigma = jax.nn.sigmoid(g)
        silu = g * sigma
        hidden = (silu * u).astype(BF16)
        total = total + jnp.sum(hidden.astype(F32) * h, axis=1, keepdims=True)
        h = h * gate
        hidden_ref[:, tile] = hidden
        grad_gate_ref[:, tile] = (h * u * sigma * (1.0 + g * (1.0 - sigma))).astype(BF16)
        grad_up_ref[:, tile] = (h * silu).astype(BF16)
    hidden_low = dot_nt(hidden_ref[...], down_ref[...]).astype(BF16)
    hl_ref[...] = hidden_low
    hlg_ref[...] = (hidden_low.astype(F32) * gate).astype(BF16)
    clg_ref[...] = (cot_low.astype(F32) * gate).astype(BF16)
    lg_ref[...] = dot_nt(grad_gate_ref[...], maps[0]).astype(BF16)
    lu_ref[...] = dot_nt(grad_up_ref[...], maps[1]).astype(BF16)
    for i in range(sources):
        line = jnp.sum(chosen[i] * total[i * cap : (i + 1) * cap], axis=0, keepdims=True)
        signed_ref[i : i + 1, :] = line * signs_ref[i : i + 1, :]


def run_middle(head, picks, after):
    rows, maps = head[0].shape[0], head[5]
    shapes = middle_shapes(rows, maps.shape[2], maps.shape[1], len(picks), picks[0].shape[1])
    return call(middle_body, head + picks, after, shapes)


def run_back(share_start, share, head, mid, rows_x, rows_c, weights, adapter_in_t, down_out, picks, totals, after, cost):
    rows, hidden_width = rows_x.shape[0], weights[0].shape[1]
    rank, features = down_out.shape
    sources = len(picks)
    cap = rows // sources
    width = hidden_width if share % 128 else share
    tile = min(256, features)
    tokens = picks[0].shape[1]

    def fixed(value):
        return pl.BlockSpec(value.shape, lambda i, n=value.ndim: (0,) * n)

    last = pl.BlockSpec((rows, tile), lambda i: (0, i))
    low = pl.BlockSpec((rank, tile), lambda i: (0, i))
    pair = pl.BlockSpec((2, rank, tile), lambda i: (0, 0, i))
    total_specs = [
        pair,
        pl.BlockSpec((2, rank, width), lambda i: (0, 0, 0)),
        pl.BlockSpec((rank, width), lambda i: (0, 0)),
        low,
    ]
    fused = mid is None
    lead = head if fused else list(mid)
    inner = middle_shapes(rows, hidden_width, rank, sources, tokens)
    args = [share_start] + lead + [rows_x, rows_c] + list(weights) + [adapter_in_t, down_out]
    args += picks + totals + after
    specs = [pl.BlockSpec(memory_space=pltpu.SMEM)] + [fixed(value) for value in lead]
    resident = pl.BlockSpec(memory_space=pltpu.VMEM)
    specs += [last, last, resident, resident, resident, pair, low] + [fixed(pick) for pick in picks]
    specs += total_specs[: len(totals)] + [pl.BlockSpec(memory_space=pl.ANY)] * len(after)
    shapes = [((2, tokens, features), BF16)] * sources
    shapes += [((2, rank, features), F32), ((2, rank, width), F32), ((rank, width), F32), ((rank, features), F32)]
    out_specs = [pl.BlockSpec((2, tokens, tile), lambda i: (0, 0, i))] * sources + total_specs
    if fused:
        shapes.append(inner[-1])
        out_specs.append(pl.BlockSpec(inner[-1][0], lambda i: (0, 0)))
    given = len(totals)
    led = 1 + len(lead)

    def body(*refs):
        start = pl.multiple_of(refs[0][0], 128) if share % 128 == 0 else 0
        x_ref, c_ref, wg, wu, wd, maps, down_ref = refs[led : led + 7]
        picks_ref = refs[led + 7 : led + 7 + sources]
        old = refs[led + 7 + sources : led + 7 + sources + given]
        outs = refs[len(args) :]
        backs, new = outs[:sources], outs[sources : sources + 4]
        middle = refs[1:led]
        if fused:
            middle = outs[sources + 5 :]

            @pl.when(pl.program_id(0) == 0)
            def _():
                middle_body(list(refs[1:led]) + list(picks_ref), list(middle) + [outs[sources + 4]])

        h_ref, gg_ref, gu_ref, hl_ref, lg_ref, lu_ref, hlg_ref, clg_ref, ag_ref, au_ref, gate_ref = middle
        lines = pl.ds(pl.multiple_of(pl.program_id(0) * tile, tile), tile)
        out = dot_nt(h_ref[...], wd[lines, :]) + SCALE * dot(hl_ref[...], down_ref[...])
        slot = (dot_nt(gg_ref[...], wg[lines, :]) + dot_nt(gu_ref[...], wu[lines, :])) + SCALE * (
            dot(lg_ref[...], maps[0]) + dot(lu_ref[...], maps[1])
        )
        for which, value in enumerate((out * gate_ref[...], slot)):
            for i in range(sources):
                part = value[i * cap : (i + 1) * cap].astype(BF16)
                backs[i][which] = dot_tn(picks_ref[i][...], part).astype(BF16)

        def add(which, index, value):
            value = SCALE * value
            if given:
                value = value + old[which][index]
            new[which][index] = value

        add(0, 0, dot_tn(lg_ref[...], x_ref[...]))
        add(0, 1, dot_tn(lu_ref[...], x_ref[...]))
        add(3, ..., dot_tn(hlg_ref[...], c_ref[...]))

        @pl.when(pl.program_id(0) == 0)
        def _():
            columns = pl.ds(start, width)
            add(1, 0, dot_tn(ag_ref[...], gg_ref[:, columns]))
            add(1, 1, dot_tn(au_ref[...], gu_ref[:, columns]))
            add(2, ..., dot_tn(clg_ref[...], h_ref[:, columns]))

    out = pl.pallas_call(
        body,
        grid=(features // tile,),
        in_specs=specs,
        out_specs=out_specs,
        out_shape=[jax.ShapeDtypeStruct(shape, dtype) for shape, dtype in shapes],
        scratch_shapes=[pltpu.VMEM(shape, dtype) for shape, dtype in inner[:-1]] if fused else [],
        compiler_params=pltpu.CompilerParams(vmem_limit_bytes=20 * 2**20),
        cost_estimate=cost,
    )(*args)
    return list(out[:sources]), list(out[sources : sources + 4]), list(out[sources + 4 :])


def run_end(backs, packs, gathered, gates, routes, router_t, after):
    token_count = backs[0].shape[1]
    experts, features = router_t.shape
    args = backs + packs + gathered + [gates, routes, router_t]
    shapes = [((token_count, features), BF16), ((token_count, features), BF16), ((experts, features), F32)]

    def body(ins, outs):
        backs_ref, packs_ref, gathered_ref = ins[:experts], ins[experts : 2 * experts], ins[2 * experts : 3 * experts]
        gates_ref, routes_ref, router_ref = ins[3 * experts :]
        number = lax.broadcasted_iota(jnp.int32, (experts, 1), 0).astype(F32)
        terms, first_line = [], None
        for i in range(experts):
            at = slice(i * token_count, (i + 1) * token_count)
            margin = sum_tree([gathered_ref[j][i ^ j : (i ^ j) + 1, :] for j in range(experts)])
            step = gates_ref[0:1, at] * gates_ref[1:2, at] * margin
            line = step * (
                (routes_ref[0:1, at] == number).astype(F32) - (routes_ref[1:2, at] == number).astype(F32)
            )
            line = line.astype(BF16)
            first_line = line if i == 0 else first_line
            terms.append(dot(line, packs_ref[i][:token_count, :features]))
        outs[2][...] = sum_tree(terms)
        outs[0][...] = sum_tree([back[0].astype(F32) for back in backs_ref]).astype(BF16)
        outs[1][...] = (
            sum_tree([back[1].astype(F32) for back in backs_ref])
            + dot_tn(first_line, router_ref[...])
        ).astype(BF16)

    return call(body, args, after, shapes, True)


def hop(value, step, count):
    return lax.ppermute(value, "expert", [(e, e ^ step) for e in range(count)])


def gather_direct(value, count):
    return [value] + [hop(value, step, count) for step in range(1, count)]


def gather_sources(value, count):
    got = [value] + [None] * (count - 1)
    bits = [1 << b for b in range(count.bit_length() - 1)]
    for index in sorted(range(1, count), key=lambda i: bin(i).count("1")):
        low_bit = index & -index
        got[index] = hop(got[index ^ low_bit], low_bit, count)
    return got


def sum_tree(values):
    while len(values) > 1:
        values = [values[2 * i] + values[2 * i + 1] for i in range(len(values) // 2)]
    return values[0]


def sum_dp(value, parts):
    if parts & (parts - 1):
        return lax.psum(value, "dp")
    step = 1
    while step < parts:
        value = value + lax.ppermute(value, "dp", [(z, z ^ step) for z in range(parts)])
        step *= 2
    return value


def shards(
    tokens,
    routes,
    router_w,
    codes,
    scales,
    adapter_in,
    adapter_out,
    down_in,
    down_out,
    cotangent,
):
    token_count, features = tokens.shape
    slots = routes.shape[1]
    experts = router_w.shape[1]
    capacity = 3 * token_count * slots // (2 * experts)
    codes, scales_t = codes[0], jnp.swapaxes(scales[0], 1, 2)
    adapter_in_t = jnp.swapaxes(adapter_in[0], 1, 2)
    adapter_out, down_out = adapter_out[0], down_out[0]
    down_in_t = down_in[0].T
    router_t = router_w.T
    hidden_width = codes.shape[1]
    blocks = scales_t.shape[1]
    parts = lax.axis_size("dp")
    me = lax.axis_index("expert").astype(F32)
    z_index = lax.axis_index("dp")
    share = hidden_width // parts
    share_start = (z_index * share).astype(jnp.int32).reshape(1)
    end = ((z_index == 0) | (z_index == parts - 1)).astype(jnp.int32).reshape(1)
    number = lax.broadcasted_iota(jnp.int32, (experts, 1), 0).astype(F32)

    table = np.zeros((8, 128), np.float32)
    table[:, :16] = np.asarray(NF4_LEVELS, np.float32)
    levels = jnp.asarray(table)
    block_of = np.arange(hidden_width) // (hidden_width // blocks)
    spread = jnp.asarray(np.arange(blocks)[:, None] == block_of[None, :], BF16)
    before = jnp.asarray(np.arange(token_count)[:, None] < np.arange(token_count)[None, :], BF16)
    row_number = jnp.asarray(np.arange(capacity)[:, None], F32)
    weights = [dequantize(codes, scales_t, levels, spread, 0), None, None]

    per_chunk = max(1, experts // 4)
    order = [list(range(i, i + per_chunk)) for i in range(0, experts, per_chunk)]
    if len(order) == 4:
        order = [order[0], order[2], order[3], order[1]]

    def picks_of(first, second):
        mine = (first == me) | (second == me)
        pad = jnp.concatenate([mine, mine, mine, mine, mine, mine, mine, mine], axis=0)
        place = dot(pad[: max(8, mine.shape[0])].astype(BF16), before)
        return [
            (mine[i : i + 1] & (place[i : i + 1] == row_number)).astype(BF16) for i in range(mine.shape[0])
        ]

    routes_t = routes.T.astype(F32)
    picks = picks_of(routes_t[0:1], routes_t[1:2])
    routes_pad = jnp.pad(routes_t.astype(BF16), ((0, 14), (0, 0)))
    packs, chunk_x, chunk_c, shared = [], {}, {}, {}

    def spread_start(packed):
        packs[:] = gather_sources(packed, experts)
        rows = [pack[token_count : token_count + 2, :token_count].astype(F32) for pack in packs]
        shared["routes"] = jnp.concatenate(rows, axis=1)
        if experts > 1:
            first = jnp.concatenate([row[0:1] for row in rows[1:]], axis=0)
            second = jnp.concatenate([row[1:2] for row in rows[1:]], axis=0)
            picks[1:] = picks_of(first, second)

    def settle_gates(logits, more, after):
        first = (shared["routes"][0:1] == me).astype(F32)
        args = [logits] + ([more] if more is not None else []) + [shared["routes"], first]
        row = ((1, first.shape[1]), F32)

        def body(ins, outs):
            total = ins[0][...] + (ins[1][...] if more is not None else 0.0)
            routes_ref, first_ref = ins[-2:]
            which = lax.broadcasted_iota(jnp.int32, (experts, 1), 0).astype(F32)
            chosen = [
                jnp.sum(jnp.where(routes_ref[k : k + 1, :] == which, total, 0.0), axis=0, keepdims=True)
                for k in range(2)
            ]
            margin = chosen[0] - chosen[1]
            gate, other = jax.nn.sigmoid(margin), jax.nn.sigmoid(-margin)
            outs[0][0:1, :] = gate
            outs[0][1:2, :] = other
            mine = first_ref[...] > 0.5
            outs[1][...] = jnp.where(mine, gate, other)
            outs[2][...] = jnp.where(mine, 1.0, -1.0)

        out = call(body, args, after, [((2, first.shape[1]), F32), row, row])
        shared["gates"] = out[0]
        shared["mine"] = out[1].reshape(experts, token_count)
        shared["signs"] = out[2].reshape(experts, token_count)

    def step(n, j, pairs, after, logits=False):
        kind, unit, pack = None, None, None
        if n is not None:
            kind = j
            if weights[j] is None:
                weights[j] = dequantize(codes, scales_t, levels, spread, j, *after)
            if j == 0:
                taken = [(picks[i], packs[i] if packs else tokens, 0) for i in order[n]]
                unit = (None, taken, weights[0], adapter_in_t)
            elif j == 1:
                unit = (chunk_x[n], None, weights[1], adapter_in_t)
            else:
                unit = (None, [(picks[i], packs[i], features) for i in order[n]], weights[2], down_out)
            if j == 0 and not packs:
                pack = (tokens, cotangent, routes_pad)
        logits_of = (router_t, packs) if logits else None
        out = run_step(end, kind, unit, pairs, pack, logits_of, after)
        if logits:
            shared["logits"] = out.pop()
        if pack is not None:
            spread_start(out.pop())
        term = None
        if kind is not None:
            if kind == 0:
                chunk_x[n] = out.pop(0)
            elif kind == 2:
                chunk_c[n] = out.pop(0)
            term = out.pop(0)
        return term, dict(zip(pairs, out))

    back, totals, signed, waiting = {}, [], {}, {}

    def finish(n, sums, after, split=False):
        chosen = [picks[i] for i in order[n]]
        gates = jnp.concatenate([shared["mine"][i : i + 1] for i in order[n]], axis=0)
        signs = jnp.concatenate([shared["signs"][i : i + 1] for i in order[n]], axis=0)
        head = list(sums) + [gates, signs, adapter_out, down_in_t]
        mid, cost = None, NO_COST
        if split:
            mid = run_middle(head, chosen, after)
            lines, after, cost = [mid.pop()], [mid[0]], LAST_COST
        dense, new, extra = run_back(
            share_start,
            share,
            head,
            mid,
            chunk_x[n],
            chunk_c[n],
            weights,
            adapter_in_t,
            down_out,
            chosen,
            totals,
            after,
            cost,
        )
        lines = lines if split else extra
        totals[:] = new
        for at, i in enumerate(order[n]):
            signed[i] = lines[0][at : at + 1]
            waiting[i] = dense[at]
        return [new[0]]

    def send_back(n):
        for i in order[n]:
            value = waiting[i]
            if i:
                value = hop(value, i, experts)
            back[i] = value

    chunks = len(order)
    units = [(n, j) for n in range(chunks) for j in range(3)]
    total = len(units)
    after = []
    if parts == 4 and per_chunk == 1:
        term, near, inner, far, carried, final = {}, {}, {}, {}, {}, {}
        for t in range(total + 3 * LAG):
            old = t - LAG
            pairs = {}
            if 0 <= t - LAG < total:
                pairs["b"] = (term[old], near[old])
            if 0 <= t - 2 * LAG < total:
                pairs["c"] = (inner[old], far[old])
            if 0 <= t - 3 * LAG < total:
                pairs["d"] = (carried[old], near[old])
            n, j = units[t] if t < total else (None, None)
            if t == 8:
                pairs["e"] = (shared["logits"], nearby)
            new, sums = step(n, j, pairs, after, logits=t == 6)
            if t == 6:
                nearby = lax.ppermute(shared["logits"], "dp", [(z, z ^ 1) for z in range(4)])
            if t == 8:
                shared["logits"] = sums.pop("e")
                distant = lax.ppermute(shared["logits"], "dp", [(z, z ^ 2) for z in range(4)])
            if new is not None:
                term[t] = new
            if "c" in sums:
                carried[t] = sums["c"]
                way = (INWARD if new is not None else []) + OUTWARD
                near[t] = lax.ppermute(carried[t], "dp", way)
            elif new is not None:
                near[t] = lax.ppermute(new, "dp", INWARD)
            if "b" in sums:
                inner[t] = sums["b"]
                far[t] = lax.ppermute(inner[t], "dp", MIDDLE)
            after = [new if new is not None else list(sums.values())[0]]
            if "d" in sums:
                final[t - 3 * LAG] = sums["d"]
            for m in range(chunks):
                wait = (2, 3, 1, 0)[m]
                if t == 3 * m + 2 + 3 * LAG + wait:
                    if m == 0:
                        settle_gates(shared["logits"], distant, after)
                    last = m == chunks - 1
                    after = finish(m, [final[3 * m + f] for f in range(3)], after, last)
                    send_back(m)
    else:
        top = jnp.concatenate([tokens, cotangent], axis=1)
        low = jnp.pad(routes_pad, ((0, 0), (0, 2 * features - token_count)))
        spread_start(jnp.concatenate([top, low], axis=0))
        sums = {}
        for n, j in units:
            new = step(n, j, {}, after)[0]
            after = [new]
            sums[n, j] = lax.psum(new, "dp")
        step(None, None, {}, after, logits=True)
        settle_gates(sum_dp(shared["logits"], parts), None, [])
        for n in range(chunks):
            after = finish(n, [sums[n, j] for j in range(3)], after)
            send_back(n)

    gathered = gather_direct(jnp.concatenate([signed[i] for i in range(experts)], axis=0), experts)
    out_y, grad_tokens, grad_router = run_end(
        [back[i] for i in range(experts)], packs, gathered, shared["gates"], shared["routes"], router_t, after
    )
    grad_a, grad_b, grad_di, grad_do = totals
    if share % 128:
        grad_b = lax.dynamic_slice_in_dim(grad_b, z_index * share, share, 2)
        grad_di = lax.dynamic_slice_in_dim(grad_di, z_index * share, share, 1)
    return (
        out_y,
        grad_tokens,
        grad_router.T,
        jnp.swapaxes(grad_a, 1, 2)[None],
        grad_b[None],
        grad_di.T[None],
        grad_do[None],
    )


def solution(mesh):
    in_specs = (
        P(("groups", "expert"), "dp"),
        P(("groups", "expert"), None),
        P("dp", None),
        P("expert", "dp", None),
        P("expert", None, "dp", None),
        P("expert", None, "dp", None),
        P("expert", None, None, None),
        P("expert", None, None),
        P("expert", None, "dp"),
        P(("groups", "expert"), "dp"),
    )
    out_specs = (
        P(("groups", "expert"), "dp"),
        P(("groups", "expert"), "dp"),
        P(("groups", "dp"), None),
        P(("groups", "expert"), None, "dp", None),
        P(("groups", "expert"), None, None, "dp"),
        P(("groups", "expert"), "dp", None),
        P(("groups", "expert"), None, "dp"),
    )
    return jax.shard_map(shards, mesh=mesh, in_specs=in_specs, out_specs=out_specs, check_vma=False)
```

```python
import functools

import jax
import jax.numpy as jnp
import numpy as np
from jax import lax
from jax.experimental import pallas as pl
from jax.experimental.pallas import tpu as pltpu
from jax.sharding import PartitionSpec as P

NF4_LEVELS = (
    -1.0,
    -0.6961928009986877,
    -0.5250730514526367,
    -0.39491748809814453,
    -0.28444138169288635,
    -0.18477343022823334,
    -0.09105003625154495,
    0.0,
    0.07958029955625534,
    0.16093020141124725,
    0.24611230194568634,
    0.3379152424240112,
    0.44070982933044434,
    0.5626170039176941,
    0.7229568362236023,
    1.0,
)
SCALE = 0.5
BF16 = jnp.bfloat16
F32 = jnp.float32
LAG = 2
LAST_COST = pl.CostEstimate(flops=6 * 10**9, bytes_accessed=16 * 10**6, transcendentals=0)
NO_COST = pl.CostEstimate(flops=0, bytes_accessed=0, transcendentals=0)
INWARD = [(0, 1), (3, 2)]
MIDDLE = [(1, 2), (2, 1)]
OUTWARD = [(1, 0), (2, 3)]


def dot(left, right):
    return jnp.dot(left, right, preferred_element_type=F32)


def dot_tn(left, right):
    return lax.dot_general(left, right, (((0,), (0,)), ((), ())), preferred_element_type=F32)


def dot_nt(left, right):
    return lax.dot_general(left, right, (((1,), (1,)), ((), ())), preferred_element_type=F32)


def select_level(code):
    found = list(NF4_LEVELS)
    for bit in range(4):
        odd = (code & (1 << bit)) != 0
        found = [jnp.where(odd, found[2 * i + 1], found[2 * i]) for i in range(len(found) // 2)]
    return found[0]


def dequantize_kernel(code_ref, scale_ref, level_ref, spread_ref, *refs, field):
    out_ref = refs[-1]
    rows, width = code_ref.shape
    step = 64
    table = jnp.broadcast_to(level_ref[0:1, :], (step, 128))
    scales = scale_ref[0]
    high = scales.astype(BF16)
    rest = scales - high.astype(F32)
    middle = rest.astype(BF16)
    low = (rest - middle.astype(F32)).astype(BF16)
    for column in range(0, width, 128):
        spread = spread_ref[:, column : column + 128]
        wide = (dot_tn(high, spread) + dot_tn(middle, spread)) + dot_tn(low, spread)
        for row in range(0, rows, step):
            code = (code_ref[row : row + step, column : column + 128] >> (4 * field)) & 15
            if column // 128 % 3 == 1:
                level = select_level(code)
            else:
                level = jnp.take_along_axis(table, code, axis=1)
            out_ref[row : row + step, column : column + 128] = (
                level * wide[row : row + step]
            ).astype(BF16)


def dequantize(codes, scales, levels, spread, field, *after):
    features, width = codes.shape
    blocks = scales.shape[1]
    rows = min(256, features)
    return pl.pallas_call(
        functools.partial(dequantize_kernel, field=field),
        grid=(features // rows,),
        in_specs=[
            pl.BlockSpec((rows, width), lambda i: (i, 0)),
            pl.BlockSpec((1, blocks, rows), lambda i: (field, 0, i)),
            pl.BlockSpec((8, 128), lambda i: (0, 0)),
            pl.BlockSpec((blocks, width), lambda i: (0, 0)),
        ]
        + [pl.BlockSpec(memory_space=pl.ANY)] * len(after),
        out_specs=pl.BlockSpec((rows, width), lambda i: (i, 0)),
        out_shape=jax.ShapeDtypeStruct((features, width), BF16),
        compiler_params=pltpu.CompilerParams(vmem_limit_bytes=(12 if after else 56) * 2**20),
        cost_estimate=NO_COST,
    )(codes, scales, levels, spread, *after)


def call(body, args, after, shapes, piped=False, limit=24):
    smem = pl.BlockSpec(memory_space=pltpu.SMEM)
    count = len(args)
    extra = len(after)

    def whole(shape):
        if piped:
            return pl.BlockSpec(shape, lambda i: (0,) * len(shape))
        return pl.BlockSpec(memory_space=pltpu.VMEM)

    def kernel(*refs):
        body(list(refs[:count]), list(refs[count + extra :]))

    out = pl.pallas_call(
        kernel,
        grid=(1,) if piped else (),
        in_specs=[smem if a.dtype == jnp.int32 else whole(a.shape) for a in args]
        + [pl.BlockSpec(memory_space=pl.ANY)] * extra,
        out_specs=[whole(shape) for shape, _ in shapes],
        out_shape=[jax.ShapeDtypeStruct(shape, dtype) for shape, dtype in shapes],
        compiler_params=pltpu.CompilerParams(vmem_limit_bytes=(limit if piped else 10) * 2**20),
        cost_estimate=NO_COST,
    )(*args, *after)
    return list(out)


def run_step(end, kind, unit, pairs, pack, logits_of, after):
    args, shapes, count = [end], [], 0
    if kind is not None:
        rows, blocks, weight, low = unit
        if kind == 1:
            args.append(rows)
            count = rows.shape[0]
        else:
            features = weight.shape[0]
            count = sum(pick.shape[0] for pick, _, _ in blocks)
            for pick, block, _ in blocks:
                args += [pick, block]
            shapes.append(((count, features), BF16))
        args += [weight, low]
        shapes.append(((count, weight.shape[1] + low.shape[-2]), BF16))
    for name in pairs:
        args += list(pairs[name])
        shapes.append((pairs[name][0].shape, pairs[name][0].dtype))
    if pack is not None:
        args += list(pack)
        tokens, _, routes = pack
        shapes.append(((tokens.shape[0] + routes.shape[0], 2 * tokens.shape[1]), BF16))
    if logits_of is not None:
        router, packs = logits_of
        token_count = packs[0].shape[0] - 16
        args += [router] + packs
        shapes.append(((router.shape[0], token_count * len(packs)), F32))

    def body(ins, outs):
        is_end = ins.pop(0)[0]
        term = None
        if kind is not None:
            if kind == 1:
                rows_ref = ins.pop(0)
            else:
                rows_ref = outs.pop(0)
                found = []
                for pick, block, at in blocks:
                    pick_ref, block_ref = ins.pop(0), ins.pop(0)
                    found.append(
                        dot(pick_ref[...], block_ref[: pick.shape[1], at : at + rows_ref.shape[1]])
                    )
                rows_ref[...] = (jnp.concatenate(found, axis=0) if len(found) > 1 else found[0]).astype(
                    BF16
                )
            weight_ref, low_ref = ins.pop(0), ins.pop(0)
            term = outs.pop(0)
            width = weight_ref.shape[1]
            for column in range(0, width, 512):
                tile = slice(column, column + 512)
                term[:, tile] = dot(rows_ref[...], weight_ref[:, tile]).astype(BF16)
            low_map = low_ref[...] if kind == 2 else low_ref[kind]
            term[:, width:] = dot_nt(rows_ref[...], low_map).astype(BF16)
        for name in pairs:
            left, right, out = ins.pop(0), ins.pop(0), outs.pop(0)
            if name in "be" or (name == "c" and term is None):
                out[...] = (left[...].astype(F32) + right[...].astype(F32)).astype(out.dtype)
            elif name == "c":

                @pl.when(is_end == 1)
                def _(out=out):
                    out[...] = term[...]

                @pl.when(is_end == 0)
                def _(out=out, left=left, right=right):
                    out[...] = (left[...].astype(F32) + right[...].astype(F32)).astype(BF16)

            else:

                @pl.when(is_end == 1)
                def _(out=out, right=right):
                    out[...] = right[...]

                @pl.when(is_end == 0)
                def _(out=out, left=left):
                    out[...] = left[...]

        if pack is not None:
            tokens_ref, cots_ref, routes_ref, out = ins.pop(0), ins.pop(0), ins.pop(0), outs.pop(0)
            top, left = tokens_ref.shape
            out[:top, :left] = tokens_ref[...]
            out[:top, left:] = cots_ref[...]
            out[top:, : routes_ref.shape[1]] = routes_ref[...]
        if logits_of is not None:
            router_ref, out = ins.pop(0), outs.pop(0)
            features = router_ref.shape[1]
            for number in range(len(packs)):
                block = ins.pop(0)
                out[:, number * token_count : (number + 1) * token_count] = dot_nt(
                    router_ref[...], block[:token_count, :features]
                )

    return call(body, args, after, shapes)


def middle_shapes(rows, hidden_width, rank, sources, tokens):
    wide, low = ((rows, hidden_width), BF16), ((rows, rank), BF16)
    return [wide, wide, wide] + [low] * 7 + [((rows, 1), F32), ((sources, tokens), F32)]


def middle_body(ins, outs):
    gate_ref, up_ref, cot_ref, gates_ref, signs_ref, maps, down_ref = ins[:7]
    picks_ref = ins[7:]
    sources = len(picks_ref)
    rows = gate_ref.shape[0]
    cap = rows // sources
    hidden_width = maps.shape[2]
    hidden_ref, grad_gate_ref, grad_up_ref, hl_ref, lg_ref, lu_ref, hlg_ref, clg_ref = outs[:8]
    ag_ref, au_ref, gate_out, signed_ref = outs[8:]
    ag_ref[...] = gate_ref[:, hidden_width:]
    au_ref[...] = up_ref[:, hidden_width:]
    chosen = [pick[...].astype(F32) for pick in picks_ref]
    gate = [jnp.sum(chosen[i] * gates_ref[i : i + 1, :], axis=1, keepdims=True) for i in range(sources)]
    gate = jnp.concatenate(gate, axis=0) if sources > 1 else gate[0]
    gate_out[...] = gate
    cot_low = cot_ref[:, hidden_width:]
    total = jnp.zeros((rows, 1), F32)
    step = 512
    for column in range(0, hidden_width, step):
        tile = slice(column, column + step)
        g = gate_ref[:, tile].astype(F32) + SCALE * dot(gate_ref[:, hidden_width:], maps[0, :, tile])
        u = up_ref[:, tile].astype(F32) + SCALE * dot(up_ref[:, hidden_width:], maps[1, :, tile])
        h = cot_ref[:, tile].astype(F32) + SCALE * dot(cot_low, down_ref[:, tile])
        sigma = jax.nn.sigmoid(g)
        silu = g * sigma
        hidden = (silu * u).astype(BF16)
        total = total + jnp.sum(hidden.astype(F32) * h, axis=1, keepdims=True)
        h = h * gate
        hidden_ref[:, tile] = hidden
        grad_gate_ref[:, tile] = (h * u * sigma * (1.0 + g * (1.0 - sigma))).astype(BF16)
        grad_up_ref[:, tile] = (h * silu).astype(BF16)
    hidden_low = dot_nt(hidden_ref[...], down_ref[...]).astype(BF16)
    hl_ref[...] = hidden_low
    hlg_ref[...] = (hidden_low.astype(F32) * gate).astype(BF16)
    clg_ref[...] = (cot_low.astype(F32) * gate).astype(BF16)
    lg_ref[...] = dot_nt(grad_gate_ref[...], maps[0]).astype(BF16)
    lu_ref[...] = dot_nt(grad_up_ref[...], maps[1]).astype(BF16)
    for i in range(sources):
        line = jnp.sum(chosen[i] * total[i * cap : (i + 1) * cap], axis=0, keepdims=True)
        signed_ref[i : i + 1, :] = line * signs_ref[i : i + 1, :]


def run_middle(head, picks, after):
    rows, maps = head[0].shape[0], head[5]
    shapes = middle_shapes(rows, maps.shape[2], maps.shape[1], len(picks), picks[0].shape[1])
    return call(middle_body, head + picks, after, shapes)


def run_back(share_start, share, head, mid, rows_x, rows_c, weights, adapter_in_t, down_out, picks, totals, after, cost):
    rows, hidden_width = rows_x.shape[0], weights[0].shape[1]
    rank, features = down_out.shape
    sources = len(picks)
    cap = rows // sources
    width = hidden_width if share % 128 else share
    tile = min(512, features)
    tokens = picks[0].shape[1]

    def fixed(value):
        return pl.BlockSpec(value.shape, lambda i, n=value.ndim: (0,) * n)

    last = pl.BlockSpec((rows, tile), lambda i: (0, i))
    low = pl.BlockSpec((rank, tile), lambda i: (0, i))
    pair = pl.BlockSpec((2, rank, tile), lambda i: (0, 0, i))
    total_specs = [
        pair,
        pl.BlockSpec((2, rank, width), lambda i: (0, 0, 0)),
        pl.BlockSpec((rank, width), lambda i: (0, 0)),
        low,
    ]
    fused = mid is None
    lead = head if fused else list(mid)
    inner = middle_shapes(rows, hidden_width, rank, sources, tokens)
    args = [share_start] + lead + [rows_x, rows_c] + list(weights) + [adapter_in_t, down_out]
    args += picks + totals + after
    specs = [pl.BlockSpec(memory_space=pltpu.SMEM)] + [fixed(value) for value in lead]
    resident = pl.BlockSpec(memory_space=pltpu.VMEM)
    specs += [last, last, resident, resident, resident, pair, low] + [fixed(pick) for pick in picks]
    specs += total_specs[: len(totals)] + [pl.BlockSpec(memory_space=pl.ANY)] * len(after)
    shapes = [((2, tokens, features), BF16)] * sources
    shapes += [((2, rank, features), F32), ((2, rank, width), F32), ((rank, width), F32), ((rank, features), F32)]
    out_specs = [pl.BlockSpec((2, tokens, tile), lambda i: (0, 0, i))] * sources + total_specs
    if fused:
        shapes.append(inner[-1])
        out_specs.append(pl.BlockSpec(inner[-1][0], lambda i: (0, 0)))
    given = len(totals)
    led = 1 + len(lead)

    def body(*refs):
        start = pl.multiple_of(refs[0][0], 128) if share % 128 == 0 else 0
        x_ref, c_ref, wg, wu, wd, maps, down_ref = refs[led : led + 7]
        picks_ref = refs[led + 7 : led + 7 + sources]
        old = refs[led + 7 + sources : led + 7 + sources + given]
        outs = refs[len(args) :]
        backs, new = outs[:sources], outs[sources : sources + 4]
        middle = refs[1:led]
        if fused:
            middle = outs[sources + 5 :]

            @pl.when(pl.program_id(0) == 0)
            def _():
                middle_body(list(refs[1:led]) + list(picks_ref), list(middle) + [outs[sources + 4]])

        h_ref, gg_ref, gu_ref, hl_ref, lg_ref, lu_ref, hlg_ref, clg_ref, ag_ref, au_ref, gate_ref = middle
        lines = pl.ds(pl.multiple_of(pl.program_id(0) * tile, tile), tile)
        out = dot_nt(h_ref[...], wd[lines, :]) + SCALE * dot(hl_ref[...], down_ref[...])
        slot = (dot_nt(gg_ref[...], wg[lines, :]) + dot_nt(gu_ref[...], wu[lines, :])) + SCALE * (
            dot(lg_ref[...], maps[0]) + dot(lu_ref[...], maps[1])
        )
        for which, value in enumerate((out * gate_ref[...], slot)):
            for i in range(sources):
                part = value[i * cap : (i + 1) * cap].astype(BF16)
                backs[i][which] = dot_tn(picks_ref[i][...], part).astype(BF16)

        def add(which, index, value):
            value = SCALE * value
            if given:
                value = value + old[which][index]
            new[which][index] = value

        add(0, 0, dot_tn(lg_ref[...], x_ref[...]))
        add(0, 1, dot_tn(lu_ref[...], x_ref[...]))
        add(3, ..., dot_tn(hlg_ref[...], c_ref[...]))

        @pl.when(pl.program_id(0) == 0)
        def _():
            columns = pl.ds(start, width)
            add(1, 0, dot_tn(ag_ref[...], gg_ref[:, columns]))
            add(1, 1, dot_tn(au_ref[...], gu_ref[:, columns]))
            add(2, ..., dot_tn(clg_ref[...], h_ref[:, columns]))

    out = pl.pallas_call(
        body,
        grid=(features // tile,),
        in_specs=specs,
        out_specs=out_specs,
        out_shape=[jax.ShapeDtypeStruct(shape, dtype) for shape, dtype in shapes],
        scratch_shapes=[pltpu.VMEM(shape, dtype) for shape, dtype in inner[:-1]] if fused else [],
        compiler_params=pltpu.CompilerParams(vmem_limit_bytes=20 * 2**20),
        cost_estimate=cost,
    )(*args)
    return list(out[:sources]), list(out[sources : sources + 4]), list(out[sources + 4 :])


def run_end(backs, packs, gathered, gates, routes, router_t, after):
    token_count = backs[0].shape[1]
    experts, features = router_t.shape
    args = backs + packs + gathered + [gates, routes, router_t]
    shapes = [((token_count, features), BF16), ((token_count, features), BF16), ((experts, features), F32)]

    def body(ins, outs):
        backs_ref, packs_ref, gathered_ref = ins[:experts], ins[experts : 2 * experts], ins[2 * experts : 3 * experts]
        gates_ref, routes_ref, router_ref = ins[3 * experts :]
        number = lax.broadcasted_iota(jnp.int32, (experts, 1), 0).astype(F32)
        terms, first_line = [], None
        for i in range(experts):
            at = slice(i * token_count, (i + 1) * token_count)
            margin = sum_tree([gathered_ref[j][i ^ j : (i ^ j) + 1, :] for j in range(experts)])
            step = gates_ref[0:1, at] * gates_ref[1:2, at] * margin
            line = step * (
                (routes_ref[0:1, at] == number).astype(F32) - (routes_ref[1:2, at] == number).astype(F32)
            )
            line = line.astype(BF16)
            first_line = line if i == 0 else first_line
            terms.append(dot(line, packs_ref[i][:token_count, :features]))
        outs[2][...] = sum_tree(terms)
        outs[0][...] = sum_tree([back[0].astype(F32) for back in backs_ref]).astype(BF16)
        outs[1][...] = (
            sum_tree([back[1].astype(F32) for back in backs_ref])
            + dot_tn(first_line, router_ref[...])
        ).astype(BF16)

    return call(body, args, after, shapes, True)


def hop(value, step, count):
    return lax.ppermute(value, "expert", [(e, e ^ step) for e in range(count)])


def gather_direct(value, count):
    return [value] + [hop(value, step, count) for step in range(1, count)]


def gather_sources(value, count):
    got = [value] + [None] * (count - 1)
    bits = [1 << b for b in range(count.bit_length() - 1)]
    for index in sorted(range(1, count), key=lambda i: bin(i).count("1")):
        low_bit = index & -index
        got[index] = hop(got[index ^ low_bit], low_bit, count)
    return got


def sum_tree(values):
    while len(values) > 1:
        values = [values[2 * i] + values[2 * i + 1] for i in range(len(values) // 2)]
    return values[0]


def sum_dp(value, parts):
    if parts & (parts - 1):
        return lax.psum(value, "dp")
    step = 1
    while step < parts:
        value = value + lax.ppermute(value, "dp", [(z, z ^ step) for z in range(parts)])
        step *= 2
    return value


def shards(
    tokens,
    routes,
    router_w,
    codes,
    scales,
    adapter_in,
    adapter_out,
    down_in,
    down_out,
    cotangent,
):
    token_count, features = tokens.shape
    slots = routes.shape[1]
    experts = router_w.shape[1]
    capacity = 3 * token_count * slots // (2 * experts)
    codes, scales_t = codes[0], jnp.swapaxes(scales[0], 1, 2)
    adapter_in_t = jnp.swapaxes(adapter_in[0], 1, 2)
    adapter_out, down_out = adapter_out[0], down_out[0]
    down_in_t = down_in[0].T
    router_t = router_w.T
    hidden_width = codes.shape[1]
    blocks = scales_t.shape[1]
    parts = lax.axis_size("dp")
    me = lax.axis_index("expert").astype(F32)
    z_index = lax.axis_index("dp")
    share = hidden_width // parts
    share_start = (z_index * share).astype(jnp.int32).reshape(1)
    end = ((z_index == 0) | (z_index == parts - 1)).astype(jnp.int32).reshape(1)
    number = lax.broadcasted_iota(jnp.int32, (experts, 1), 0).astype(F32)

    table = np.zeros((8, 128), np.float32)
    table[:, :16] = np.asarray(NF4_LEVELS, np.float32)
    levels = jnp.asarray(table)
    block_of = np.arange(hidden_width) // (hidden_width // blocks)
    spread = jnp.asarray(np.arange(blocks)[:, None] == block_of[None, :], BF16)
    before = jnp.asarray(np.arange(token_count)[:, None] < np.arange(token_count)[None, :], BF16)
    row_number = jnp.asarray(np.arange(capacity)[:, None], F32)
    weights = [dequantize(codes, scales_t, levels, spread, 0), None, None]

    per_chunk = max(1, experts // 4)
    order = [list(range(i, i + per_chunk)) for i in range(0, experts, per_chunk)]
    if len(order) == 4:
        order = [order[0], order[2], order[3], order[1]]

    def picks_of(first, second):
        mine = (first == me) | (second == me)
        pad = jnp.concatenate([mine, mine, mine, mine, mine, mine, mine, mine], axis=0)
        place = dot(pad[: max(8, mine.shape[0])].astype(BF16), before)
        return [
            (mine[i : i + 1] & (place[i : i + 1] == row_number)).astype(BF16) for i in range(mine.shape[0])
        ]

    routes_t = routes.T.astype(F32)
    picks = picks_of(routes_t[0:1], routes_t[1:2])
    routes_pad = jnp.pad(routes_t.astype(BF16), ((0, 14), (0, 0)))
    packs, chunk_x, chunk_c, shared = [], {}, {}, {}

    def spread_start(packed):
        packs[:] = gather_sources(packed, experts)
        rows = [pack[token_count : token_count + 2, :token_count].astype(F32) for pack in packs]
        shared["routes"] = jnp.concatenate(rows, axis=1)
        if experts > 1:
            first = jnp.concatenate([row[0:1] for row in rows[1:]], axis=0)
            second = jnp.concatenate([row[1:2] for row in rows[1:]], axis=0)
            picks[1:] = picks_of(first, second)

    def settle_gates(logits, more, after):
        first = (shared["routes"][0:1] == me).astype(F32)
        args = [logits] + ([more] if more is not None else []) + [shared["routes"], first]
        row = ((1, first.shape[1]), F32)

        def body(ins, outs):
            total = ins[0][...] + (ins[1][...] if more is not None else 0.0)
            routes_ref, first_ref = ins[-2:]
            which = lax.broadcasted_iota(jnp.int32, (experts, 1), 0).astype(F32)
            chosen = [
                jnp.sum(jnp.where(routes_ref[k : k + 1, :] == which, total, 0.0), axis=0, keepdims=True)
                for k in range(2)
            ]
            margin = chosen[0] - chosen[1]
            gate, other = jax.nn.sigmoid(margin), jax.nn.sigmoid(-margin)
            outs[0][0:1, :] = gate
            outs[0][1:2, :] = other
            mine = first_ref[...] > 0.5
            outs[1][...] = jnp.where(mine, gate, other)
            outs[2][...] = jnp.where(mine, 1.0, -1.0)

        out = call(body, args, after, [((2, first.shape[1]), F32), row, row])
        shared["gates"] = out[0]
        shared["mine"] = out[1].reshape(experts, token_count)
        shared["signs"] = out[2].reshape(experts, token_count)

    def step(n, j, pairs, after, logits=False):
        kind, unit, pack = None, None, None
        if n is not None:
            kind = j
            if weights[j] is None:
                weights[j] = dequantize(codes, scales_t, levels, spread, j, *after)
            if j == 0:
                taken = [(picks[i], packs[i] if packs else tokens, 0) for i in order[n]]
                unit = (None, taken, weights[0], adapter_in_t)
            elif j == 1:
                unit = (chunk_x[n], None, weights[1], adapter_in_t)
            else:
                unit = (None, [(picks[i], packs[i], features) for i in order[n]], weights[2], down_out)
            if j == 0 and not packs:
                pack = (tokens, cotangent, routes_pad)
        logits_of = (router_t, packs) if logits else None
        out = run_step(end, kind, unit, pairs, pack, logits_of, after)
        if logits:
            shared["logits"] = out.pop()
        if pack is not None:
            spread_start(out.pop())
        term = None
        if kind is not None:
            if kind == 0:
                chunk_x[n] = out.pop(0)
            elif kind == 2:
                chunk_c[n] = out.pop(0)
            term = out.pop(0)
        return term, dict(zip(pairs, out))

    back, totals, signed, waiting = {}, [], {}, {}

    def finish(n, sums, after, split=False):
        chosen = [picks[i] for i in order[n]]
        gates = jnp.concatenate([shared["mine"][i : i + 1] for i in order[n]], axis=0)
        signs = jnp.concatenate([shared["signs"][i : i + 1] for i in order[n]], axis=0)
        head = list(sums) + [gates, signs, adapter_out, down_in_t]
        mid, cost = None, NO_COST
        if split:
            mid = run_middle(head, chosen, after)
            lines, after, cost = [mid.pop()], [mid[0]], LAST_COST
        dense, new, extra = run_back(
            share_start,
            share,
            head,
            mid,
            chunk_x[n],
            chunk_c[n],
            weights,
            adapter_in_t,
            down_out,
            chosen,
            totals,
            after,
            cost,
        )
        lines = lines if split else extra
        totals[:] = new
        for at, i in enumerate(order[n]):
            signed[i] = lines[0][at : at + 1]
            waiting[i] = dense[at]
        return [new[0]]

    def send_back(n):
        for i in order[n]:
            value = waiting[i]
            if i:
                value = hop(value, i, experts)
            back[i] = value

    chunks = len(order)
    units = [(n, j) for n in range(chunks) for j in range(3)]
    total = len(units)
    after = []
    if parts == 4 and per_chunk == 1:
        term, near, inner, far, carried, final = {}, {}, {}, {}, {}, {}
        for t in range(total + 3 * LAG):
            old = t - LAG
            pairs = {}
            if 0 <= t - LAG < total:
                pairs["b"] = (term[old], near[old])
            if 0 <= t - 2 * LAG < total:
                pairs["c"] = (inner[old], far[old])
            if 0 <= t - 3 * LAG < total:
                pairs["d"] = (carried[old], near[old])
            n, j = units[t] if t < total else (None, None)
            if t == 8:
                pairs["e"] = (shared["logits"], nearby)
            new, sums = step(n, j, pairs, after, logits=t == 6)
            if t == 6:
                nearby = lax.ppermute(shared["logits"], "dp", [(z, z ^ 1) for z in range(4)])
            if t == 8:
                shared["logits"] = sums.pop("e")
                distant = lax.ppermute(shared["logits"], "dp", [(z, z ^ 2) for z in range(4)])
            if new is not None:
                term[t] = new
            if "c" in sums:
                carried[t] = sums["c"]
                way = (INWARD if new is not None else []) + OUTWARD
                near[t] = lax.ppermute(carried[t], "dp", way)
            elif new is not None:
                near[t] = lax.ppermute(new, "dp", INWARD)
            if "b" in sums:
                inner[t] = sums["b"]
                far[t] = lax.ppermute(inner[t], "dp", MIDDLE)
            after = [new if new is not None else list(sums.values())[0]]
            if "d" in sums:
                final[t - 3 * LAG] = sums["d"]
            for m in range(chunks):
                wait = (2, 3, 1, 0)[m]
                if t == 3 * m + 2 + 3 * LAG + wait:
                    if m == 0:
                        settle_gates(shared["logits"], distant, after)
                    last = m == chunks - 1
                    after = finish(m, [final[3 * m + f] for f in range(3)], after, last)
                    send_back(m)
    else:
        top = jnp.concatenate([tokens, cotangent], axis=1)
        low = jnp.pad(routes_pad, ((0, 0), (0, 2 * features - token_count)))
        spread_start(jnp.concatenate([top, low], axis=0))
        sums = {}
        for n, j in units:
            new = step(n, j, {}, after)[0]
            after = [new]
            sums[n, j] = lax.psum(new, "dp")
        step(None, None, {}, after, logits=True)
        settle_gates(sum_dp(shared["logits"], parts), None, [])
        for n in range(chunks):
            after = finish(n, [sums[n, j] for j in range(3)], after)
            send_back(n)

    gathered = gather_direct(jnp.concatenate([signed[i] for i in range(experts)], axis=0), experts)
    out_y, grad_tokens, grad_router = run_end(
        [back[i] for i in range(experts)], packs, gathered, shared["gates"], shared["routes"], router_t, after
    )
    grad_a, grad_b, grad_di, grad_do = totals
    if share % 128:
        grad_b = lax.dynamic_slice_in_dim(grad_b, z_index * share, share, 2)
        grad_di = lax.dynamic_slice_in_dim(grad_di, z_index * share, share, 1)
    return (
        out_y,
        grad_tokens,
        grad_router.T,
        jnp.swapaxes(grad_a, 1, 2)[None],
        grad_b[None],
        grad_di.T[None],
        grad_do[None],
    )


def solution(mesh):
    in_specs = (
        P(("groups", "expert"), "dp"),
        P(("groups", "expert"), None),
        P("dp", None),
        P("expert", "dp", None),
        P("expert", None, "dp", None),
        P("expert", None, "dp", None),
        P("expert", None, None, None),
        P("expert", None, None),
        P("expert", None, "dp"),
        P(("groups", "expert"), "dp"),
    )
    out_specs = (
        P(("groups", "expert"), "dp"),
        P(("groups", "expert"), "dp"),
        P(("groups", "dp"), None),
        P(("groups", "expert"), None, "dp", None),
        P(("groups", "expert"), None, None, "dp"),
        P(("groups", "expert"), "dp", None),
        P(("groups", "expert"), None, "dp"),
    )
    return jax.shard_map(shards, mesh=mesh, in_specs=in_specs, out_specs=out_specs, check_vma=False)
```
